128 devices in a mesh: nest: 4 (over z_lo, core), tile: 32 (over z_hi, x, y).
Axes of the slice: x: 4, y: 4, z: 4 (z_hi: 2, z_lo: 2; z = z_hi * 2 + z_lo), core: 2. Of those that a mesh axis runs over, the one named last changes fastest.
Arguments:
- nest_state: bfloat16 [4, 384, 512, 512], P('nest', None, 'tile'), may hold values from -6 to 6
- parent_state: bfloat16 [384, 16384], P(None, ('nest', 'tile')), may hold values from -6 to 6
- mix_weight: bfloat16 [384, 384], replicated, may hold values from -0.3125 to 0.3125
- intersection: int32 [4, 32, 4], P('nest', 'tile'), may hold values from 0 to 11
- interp_weight: bfloat16 [4, 32, 4, 128, 512], P('nest', 'tile'), may hold values from -0.25 to 0.25
- avg_weight: bfloat16 [4, 32, 4, 512, 128], P('nest', 'tile'), may hold values from -0.25 to 0.25
- land_mask: int32 [4, 512, 512], P('nest', 'tile'), may hold values 0 or 1
Outputs:
- nest_out: bfloat16 [4, 384, 512, 512], P('nest', None, 'tile')
- parent_out: bfloat16 [384, 16384], P(None, ('nest', 'tile'))
The draws below stay inside these ranges and needn't reach their ends.
All inputs are finite; a program needn't handle non-finite values. No bound on the sum of `land_mask` on one device may be relied on, other than what follows from the above.
Results may differ from the reference program's by a relative error of at most 0.012.
Values may be sent and summed in bfloat16 or wider, within the bound.
A program may use at most 192 MiB of HBM per device.

```python
import jax
import jax.numpy as jnp

CH = 384
CY = 16
NXN = 512
BW = 16
PT = 128
K = 4
NSUB = 2
NESTS = 4
NYN = 512
PCELLS = 16384
S2 = 512
Q = 512
N_NEST = 4
N_TILE = 32


def with_ends(array, key, least, top_value):
    shape = array.shape
    spot = [jax.random.randint(jax.random.fold_in(key, axis), (), 0, shape[axis]) for axis in range(len(shape))]
    array = array.at[tuple(spot)].set(least)
    longest = shape.index(max(shape))
    spot[longest] = (spot[longest] + 1) % shape[longest]
    return array.at[tuple(spot)].set(top_value)


def level_of(stream_key, shape, pieces, least, high):
    gain = 1.0
    for dim, shards_of in pieces:
        steps = jax.random.uniform(jax.random.fold_in(jax.random.fold_in(stream_key, 6), dim), (shards_of,), jnp.float32, least / len(pieces), high / len(pieces))
        gain = gain * jnp.repeat(jnp.exp(steps), shape[dim] // shards_of).reshape((-1,) + (1,) * (len(shape) - 1 - dim))
    return gain


def bell_draw(rng, dims, scale, limit, split=(), held_as=jnp.bfloat16):
    result = scale * jax.random.normal(rng, dims, jnp.float32)
    if split:
        result = result * level_of(rng, dims, split, -0.22, 0.18)
    return jnp.clip(result, -limit, limit).astype(held_as)


def setup_inputs(seed: int = 0) -> dict:
    arg_keys = jax.random.split(jax.random.key(seed), 8)
    return {
        "nest_state": bell_draw(arg_keys[0], (NESTS, CH, NYN, NXN), 1.0, 6.0, ((0, 4), (2, 32))),
        "parent_state": bell_draw(arg_keys[1], (CH, PCELLS), 1.0, 6.0, ((1, 128),)),
        "mix_weight": bell_draw(arg_keys[2], (CH, CH), CH ** -0.5, 0.3125),
        "intersection": with_ends(jax.random.randint(arg_keys[3], (NESTS, N_TILE, K), 0, 3 * N_NEST), jax.random.fold_in(arg_keys[3], 1), 0, (3 * N_NEST) - 1).astype(jnp.int32),
        "interp_weight": bell_draw(arg_keys[4], (NESTS, N_TILE, K, PT, S2), (K * PT) ** -0.5, 0.25, ((0, 4), (1, 32))),
        "avg_weight": bell_draw(arg_keys[5], (NESTS, N_TILE, K, Q, PT), Q ** -0.5, 0.25, ((0, 4), (1, 32))),
        "land_mask": with_ends((jax.random.randint(arg_keys[6], (NESTS, NYN, NXN), 0, 3) < 1).astype(jnp.int32), jax.random.fold_in(arg_keys[6], 1), 0, 1),
    }


def laplace(padded):
    center = padded[:, 1:-1]
    cols = jnp.pad(center, ((0, 0), (0, 0), (1, 1)))
    along_rows = padded[:, 2:] + padded[:, :-2] - 2.0 * center
    along_cols = cols[:, :, 2:] + cols[:, :, :-2] - 2.0 * center
    return 0.4 * along_rows + 0.05 * along_cols


def advance(state, padded, factor, strip, mixing):
    channels = state.shape[0]
    rounded = state.astype(jnp.bfloat16)
    mixed = jnp.dot(mixing, rounded.reshape(channels, -1), preferred_element_type=jnp.float32).reshape(state.shape)
    moved = state + factor[None] * (0.5 * mixed + laplace(padded))
    zone = strip.shape[2] // 2
    ramp = (zone - jnp.arange(zone, dtype=jnp.float32)) / zone
    west = moved[:, :, :zone]
    east = moved[:, :, -zone:]
    west = west + ramp * (strip[:, :, :zone].astype(jnp.float32) - west)
    east = east + ramp[::-1] * (strip[:, :, zone:].astype(jnp.float32) - east)
    return jnp.concatenate([west, moved[:, :, zone:-zone], east], axis=2)


def reference(nest_state, parent_state, mix_weight, intersection, interp_weight, avg_weight, land_mask):
    ndev = N_NEST * N_TILE
    group = intersection // 3
    offset = intersection % 3
    tiles_idx = (jnp.arange(N_TILE, dtype=jnp.int32)[None, :, None] + offset - 1) % N_TILE
    target = (group * N_TILE + tiles_idx).astype(jnp.int32)
    parent_tiles = parent_state.reshape(CH, ndev, PT).transpose(1, 0, 2)
    picked = parent_tiles[target].astype(jnp.float32)
    strip_all = jnp.einsum("ntkmp,ntkps->ntms", picked, interp_weight.astype(jnp.float32)).astype(jnp.bfloat16)
    strip_all = strip_all.reshape(NESTS, N_TILE, CH, CY, 2 * BW).transpose(0, 2, 1, 3, 4).reshape(NESTS, CH, NYN, 2 * BW)
    outs = []
    feeds = []
    for index in range(NESTS):
        state = nest_state[index].astype(jnp.float32)
        factor = jnp.where(land_mask[index] == 1, 0.5, 1.0).astype(jnp.float32)
        for step in range(NSUB):
            padded = jnp.pad(state, ((0, 0), (1, 1), (0, 0)))
            state = advance(state, padded, factor, strip_all[index], mix_weight)
        outs.append(state.astype(jnp.bfloat16))
        coarse = state.reshape(CH, NYN // 4, 4, NXN // 4, 4).sum(axis=(2, 4)) / 16.0
        coarse = coarse.astype(jnp.bfloat16).reshape(CH, N_TILE, CY // 4, NXN // 4)
        coarse = coarse.transpose(1, 0, 2, 3).reshape(N_TILE, CH, Q).astype(jnp.float32)
        feeds.append(jnp.einsum("tmq,tkqp->tkmp", coarse, avg_weight[index].astype(jnp.float32)))
    nest_out = jnp.stack(outs)
    feed = jnp.stack(feeds).reshape(-1, CH, PT)
    increment = jax.ops.segment_sum(feed, target.reshape(-1), num_segments=ndev)
    increment = increment.transpose(1, 0, 2).reshape(CH, PCELLS)
    parent_out = (parent_state.astype(jnp.float32) + increment).astype(jnp.bfloat16)
    return nest_out, parent_out
```

```python
import functools

import jax
import jax.numpy as jnp
from jax import lax
from jax.experimental import pallas as pl
from jax.experimental.pallas import tpu as pltpu
from jax.sharding import PartitionSpec as P

BW = 16
LANES = 128
MESH = pl.DeviceIdType.MESH
f32, bf16 = jnp.float32, jnp.bfloat16


def side_sum(x):
    zero = jnp.zeros((x.shape[0], 1), x.dtype)
    return jnp.concatenate([zero, x[:, :-1]], 1) + jnp.concatenate([x[:, 1:], zero], 1)


def kernel(
    groups, tiles, parts,
    picks, nest, parent, mix, interp, avg, land,
    nest_out, parent_out,
    xin, xa, xb, ws, cand, m_v, w_v, av_v, land_v, coef, strip_v, pool_v, coarse, fb, fbs, r1, s2, r2, s3, r3, g1, p_out,
    load_sem, p_send, p_recv, h_send, h_recv, f_send, f_recv, out_sem,
):
    channels, rows, width = xin.shape
    part = channels // parts
    slots = w_v.shape[0]
    n, t = lax.axis_index("nest"), lax.axis_index("tile")
    core = n + 1 - 2 * lax.rem(n, 2)
    deep = lax.rem(n + 2, groups)
    core_deep = lax.rem(core + 2, groups)
    up, down = lax.rem(t + 1, tiles), lax.rem(t + tiles - 1, tiles)
    to_up, to_down, to_core, to_deep = (n, up), (n, down), (core, t), (deep, t)

    def remote(src, dst, send, recv, device):
        return pltpu.make_async_remote_copy(
            src_ref=src, dst_ref=dst, send_sem=send, recv_sem=recv, device_id=device, device_id_type=MESH
        )

    barrier = pltpu.get_barrier_semaphore()
    for device in (to_up, to_down, to_core, to_deep):
        pl.semaphore_signal(barrier, inc=1, device_id=device, device_id_type=MESH)

    def span(c):
        return pl.ds(c * part, part)

    x_loads = [pltpu.make_async_copy(nest.at[0, span(c)], xin.at[span(c)], load_sem.at[c]) for c in range(parts)]
    own_load = pltpu.make_async_copy(parent, cand.at[3 * n + 1], load_sem.at[parts])
    mix_load = pltpu.make_async_copy(mix, m_v, load_sem.at[parts + 1])
    land_load = pltpu.make_async_copy(land.at[0], land_v, load_sem.at[parts + 2])
    w_load = pltpu.make_async_copy(interp.at[0, 0], w_v, load_sem.at[parts + 3])
    av_load = pltpu.make_async_copy(avg.at[0, 0], av_v, load_sem.at[parts + 4])
    own_load.start()
    for load in x_loads:
        load.start()
    for load in (mix_load, land_load, w_load, av_load):
        load.start()
    own_load.wait()
    pl.semaphore_wait(barrier, 4)

    own = cand.at[3 * n + 1]
    tile_up = remote(own, cand.at[3 * n], p_send.at[0], p_recv.at[0], to_up)
    tile_down = remote(own, cand.at[3 * n + 2], p_send.at[1], p_recv.at[1], to_down)
    tile_up.start()
    tile_down.start()

    def to_groups(o):
        mine = cand.at[3 * n + o]
        return (
            remote(mine, mine, p_send.at[2 + o], p_recv.at[2 + o], to_core),
            remote(mine, mine, p_send.at[5 + o], p_recv.at[5 + o], to_deep),
        )

    group_copies = [to_groups(o) for o in range(3)]
    for copy in group_copies[1]:
        copy.start()

    def halos(state, step, c):
        k = (step * parts + c) * 2
        return (
            remote(state.at[rows, span(c)], state.at[0, span(c)], h_send.at[k], h_recv.at[k], to_up),
            remote(state.at[1, span(c)], state.at[rows + 1, span(c)], h_send.at[k + 1], h_recv.at[k + 1], to_down),
        )

    def halo_start(state, step, c):
        upward, downward = halos(state, step, c)
        pl.when(t < tiles - 1)(upward.start)
        pl.when(t > 0)(downward.start)

    def halo_arrived(state, step, c):
        upward, downward = halos(state, step, c)
        pl.when(t > 0)(upward.wait_recv)
        pl.when(t < tiles - 1)(downward.wait_recv)

    def halo_sent(state, step, c):
        upward, downward = halos(state, step, c)
        pl.when(t < tiles - 1)(upward.wait_send)
        pl.when(t > 0)(downward.wait_send)

    @pl.when(t == 0)
    def _():
        for state in (xa, xb):
            state[0] = jnp.zeros((channels, width), bf16)

    @pl.when(t == tiles - 1)
    def _():
        for state in (xa, xb):
            state[rows + 1] = jnp.zeros((channels, width), bf16)

    for c in range(parts):
        x_loads[c].wait()

        def rows_first(i, carry, c=c):
            at = pl.ds(pl.multiple_of(c * part + i * 16, 16), 16)
            xa[1 : rows + 1, at, :] = jnp.swapaxes(xin[at], 0, 1)
            return carry

        lax.fori_loop(0, part // 16, rows_first, 0)
        halo_start(xa, 0, c)

    land_load.wait()
    mix_load.wait()
    column = lax.broadcasted_iota(jnp.int32, (rows, width), 1)
    edge = jnp.minimum(column, width - 1 - column)
    ramp = jnp.maximum(BW - edge, 0).astype(f32) / BW
    factor = jnp.where(land_v[...] == 1, 0.5, 1.0)
    coef[0] = (1.0 - ramp) * (1.0 - 0.9 * factor)
    coef[1] = (1.0 - ramp) * (0.4 * factor)

    tile_up.wait_recv()
    for copy in group_copies[0]:
        copy.start()
    tile_down.wait_recv()
    for copy in group_copies[2]:
        copy.start()

    def update(src, dst, r, first, count, with_strip):
        mixed = jnp.dot(m_v[first : first + count, :], src[r + 1], preferred_element_type=f32)
        mine, around = coef[0, pl.ds(r, 1), :], coef[1, pl.ds(r, 1), :]
        for s in range(0, count, 16):
            at = slice(first + s, first + s + 16)
            x = src[r + 1, at, :]
            near = src[r, at, :] + src[r + 2, at, :] + jnp.asarray(0.125, bf16) * side_sum(x)
            y = mine * x.astype(f32) + around * (near.astype(f32) + 1.25 * mixed[s : s + 16])
            if with_strip:
                west = y[:, :LANES] + ws[r, at, :LANES]
                east = y[:, -LANES:] + ws[r, at, LANES:]
                y = jnp.concatenate([west, y[:, LANES:-LANES], east], axis=1)
            dst[r + 1, at, :] = y.astype(bf16)

    def inner_rows(src, dst, with_strip):
        def body(i, carry):
            update(src, dst, 2 * i + 1, 0, channels, with_strip)
            update(src, dst, 2 * i + 2, 0, channels, with_strip)
            return carry

        lax.fori_loop(0, (rows - 2) // 2, body, 0)

    inner_rows(xa, xb, False)

    w_load.wait()
    for o in range(3):
        group_copies[o][1].wait_recv()
    theirs = cand.at[pl.ds(3 * deep, 3)]
    onward = remote(theirs, theirs, p_send.at[8], p_recv.at[8], to_core)
    onward.start()
    for o in range(3):
        group_copies[o][0].wait_recv()
    onward.wait_recv()
    picked = jnp.concatenate([cand[picks[0, 0, k]] for k in range(slots)], axis=1)
    weights = w_v[...].reshape(slots * LANES, width)
    strip_v[...] = jnp.dot(picked, weights, preferred_element_type=f32).astype(bf16)
    lane = lax.broadcasted_iota(jnp.int32, (1, LANES), 1)
    west_ramp = jnp.maximum(BW - lane, 0).astype(f32) / BW
    east_ramp = jnp.maximum(lane - (LANES - 1 - BW), 0).astype(f32) / BW
    per = LANES // (2 * BW)

    def spread(i, carry):
        at = pl.ds(pl.multiple_of(i * 16, 16), 16)
        for r in range(rows):
            cells = strip_v[at, (r // per) * LANES : (r // per + 1) * LANES].astype(f32)
            off = (r % per) * 2 * BW
            ws[r, at, :LANES] = pltpu.roll(cells, (LANES - off) % LANES, 1) * west_ramp
            ws[r, at, LANES:] = pltpu.roll(cells, (2 * LANES - 2 * BW - off) % LANES, 1) * east_ramp
        return carry

    lax.fori_loop(0, channels // 16, spread, 0)

    def add_strip(r, carry):
        for side, at in enumerate((slice(0, LANES), slice(width - LANES, width))):
            there = xb[r + 1, :, at].astype(f32) + ws[r, :, side * LANES : (side + 1) * LANES]
            xb[r + 1, :, at] = there.astype(bf16)
        return carry

    lax.fori_loop(1, rows - 1, add_strip, 0)

    for c in range(parts):
        halo_arrived(xa, 0, c)
        update(xa, xb, 0, c * part, part, True)
        update(xa, xb, rows - 1, c * part, part, True)
        halo_start(xb, 1, c)

    inner_rows(xb, xa, True)

    av_load.wait()
    pool_row = lax.broadcasted_iota(jnp.int32, (width, LANES), 0)
    pool_col = lax.broadcasted_iota(jnp.int32, (width, LANES), 1)
    pool_v[...] = jnp.where(pool_row // 4 == pool_col, 1.0 / 16.0, 0.0).astype(bf16)

    def average(b, first, count):
        at = slice(first, first + count)
        total = xa[4 * b + 1, at, :].astype(f32)
        for j in range(1, 4):
            total = total + xa[4 * b + 1 + j, at, :].astype(f32)
        blocks = jnp.dot(total.astype(bf16), pool_v[...], preferred_element_type=f32)
        coarse[at, b * LANES : (b + 1) * LANES] = blocks.astype(bf16)

    bands = rows // 4
    for b in range(1, bands - 1):
        average(b, 0, channels)
    for k in range(slots):
        fb[k] = jnp.dot(
            coarse[:, LANES : (bands - 1) * LANES],
            av_v[k, LANES : (bands - 1) * LANES, :],
            preferred_element_type=f32,
        )

    def core_copies(c):
        return (
            remote(fbs.at[c, core], r1.at[c, 0], f_send.at[5 * c], f_recv.at[5 * c], to_core),
            remote(fbs.at[c, core_deep], r1.at[c, 1], f_send.at[5 * c + 1], f_recv.at[5 * c + 1], to_core),
        )

    def deep_copy(c):
        return remote(s2.at[c], r2.at[c], f_send.at[5 * c + 2], f_recv.at[5 * c + 2], to_deep)

    def tile_copies(c):
        return (
            remote(s3.at[c, 0], r3.at[c, 0], f_send.at[5 * c + 3], f_recv.at[5 * c + 3], to_down),
            remote(s3.at[c, 1], r3.at[c, 1], f_send.at[5 * c + 4], f_recv.at[5 * c + 4], to_up),
        )

    def out_copy(c):
        return pltpu.make_async_copy(xin.at[span(c)], nest_out.at[0, span(c)], out_sem.at[c])

    def stage_core(c):
        for copy in core_copies(c):
            copy.wait_recv()
        s2[c] = (fbs[c, deep].astype(f32) + r1[c, 1].astype(f32)).astype(bf16)
        deep_copy(c).start()

    def stage_deep(c):
        deep_copy(c).wait_recv()
        total = fbs[c, n].astype(f32) + r1[c, 0].astype(f32) + r2[c].astype(f32)
        s3[c, 0] = total[0].astype(bf16)
        s3[c, 1] = total[2].astype(bf16)
        g1[c] = total[1]
        for copy in tile_copies(c):
            copy.start()

    def stage_tile(c):
        for copy in tile_copies(c):
            copy.wait_recv()
        mine = cand[3 * n + 1, span(c), :].astype(f32)
        total = mine + (g1[c] + r3[c, 0].astype(f32) + r3[c, 1].astype(f32))
        p_out[span(c), :] = total.astype(bf16)

    for c in range(parts):
        halo_sent(xa, 0, c)
        halo_arrived(xb, 1, c)
        update(xb, xa, 0, c * part, part, True)
        update(xb, xa, rows - 1, c * part, part, True)
        average(0, c * part, part)
        average(bands - 1, c * part, part)
        at = slice(c * part, (c + 1) * part)
        terms = []
        for k in range(slots):
            first = jnp.dot(coarse[at, :LANES], av_v[k, :LANES, :], preferred_element_type=f32)
            last = jnp.dot(
                coarse[at, (bands - 1) * LANES :], av_v[k, (bands - 1) * LANES :, :], preferred_element_type=f32
            )
            terms.append(fb[k, at, :] + first + last)
        for slot in range(3 * groups):
            total = jnp.zeros((part, LANES), f32)
            for k in range(slots):
                total = total + (picks[0, 0, k] == slot).astype(f32) * terms[k]
            fbs[c, slot // 3, slot % 3] = total.astype(bf16)
        for copy in core_copies(c):
            copy.start()
        if c > 0:
            stage_core(c - 1)

        def channels_first(i, carry, c=c):
            at = pl.ds(pl.multiple_of(c * part + i * 16, 16), 16)
            xin[at] = jnp.swapaxes(xa[1 : rows + 1, at, :], 0, 1)
            return carry

        lax.fori_loop(0, part // 16, channels_first, 0)
        out_copy(c).start()
        if c > 1:
            stage_deep(c - 2)
    stage_core(parts - 1)
    for c in range(parts - 2, parts):
        stage_deep(c)
    for c in range(parts):
        stage_tile(c)
    final = pltpu.make_async_copy(p_out, parent_out, load_sem.at[parts])
    final.start()

    tile_up.wait_send()
    tile_down.wait_send()
    for pair in group_copies:
        for copy in pair:
            copy.wait_send()
    onward.wait_send()
    for c in range(parts):
        halo_sent(xb, 1, c)
        for copy in core_copies(c):
            copy.wait_send()
        deep_copy(c).wait_send()
        for copy in tile_copies(c):
            copy.wait_send()
        out_copy(c).wait()
    final.wait()


def shards(nest_state, parent_state, mix_weight, intersection, interp_weight, avg_weight, land_mask):
    _, channels, rows, width = nest_state.shape
    groups, tiles = lax.axis_size("nest"), lax.axis_size("tile")
    slots = intersection.shape[2]
    cells = parent_state.shape[1]
    parts = 3
    part = channels // parts
    hbm = pl.BlockSpec(memory_space=pl.ANY)
    return pl.pallas_call(
        functools.partial(kernel, groups, tiles, parts),
        out_shape=(
            jax.ShapeDtypeStruct(nest_state.shape, bf16),
            jax.ShapeDtypeStruct(parent_state.shape, bf16),
        ),
        in_specs=[pl.BlockSpec(memory_space=pltpu.SMEM)] + [hbm] * 6,
        out_specs=(hbm, hbm),
        scratch_shapes=[
            pltpu.VMEM((channels, rows, width), bf16),
            pltpu.VMEM((rows + 2, channels, width), bf16),
            pltpu.VMEM((rows + 2, channels, width), bf16),
            pltpu.VMEM((rows, channels, 2 * LANES), f32),
            pltpu.VMEM((3 * groups, channels, cells), bf16),
            pltpu.VMEM((channels, channels), bf16),
            pltpu.VMEM((slots, cells, width), bf16),
            pltpu.VMEM((slots, width, cells), bf16),
            pltpu.VMEM((rows, width), jnp.int32),
            pltpu.VMEM((2, rows, width), f32),
            pltpu.VMEM((channels, width), bf16),
            pltpu.VMEM((width, LANES), bf16),
            pltpu.VMEM((channels, width), bf16),
            pltpu.VMEM((slots, channels, cells), f32),
            pltpu.VMEM((parts, groups, 3, part, cells), bf16),
            pltpu.VMEM((parts, 2, 3, part, cells), bf16),
            pltpu.VMEM((parts, 3, part, cells), bf16),
            pltpu.VMEM((parts, 3, part, cells), bf16),
            pltpu.VMEM((parts, 2, part, cells), bf16),
            pltpu.VMEM((parts, 2, part, cells), bf16),
            pltpu.VMEM((parts, part, cells), f32),
            pltpu.VMEM((channels, cells), bf16),
            pltpu.SemaphoreType.DMA((parts + 5,)),
            pltpu.SemaphoreType.DMA((9,)),
            pltpu.SemaphoreType.DMA((9,)),
            pltpu.SemaphoreType.DMA((4 * parts,)),
            pltpu.SemaphoreType.DMA((4 * parts,)),
            pltpu.SemaphoreType.DMA((5 * parts,)),
            pltpu.SemaphoreType.DMA((5 * parts,)),
            pltpu.SemaphoreType.DMA((parts,)),
        ],
        compiler_params=pltpu.CompilerParams(
            collective_id=0, has_side_effects=True, vmem_limit_bytes=56 * 2**20
        ),
    )(intersection, nest_state, parent_state, mix_weight, interp_weight, avg_weight, land_mask)


def solution(mesh):
    in_specs = (
        P("nest", None, "tile", None),
        P(None, ("nest", "tile")),
        P(),
        P("nest", "tile", None),
        P("nest", "tile", None, None, None),
        P("nest", "tile", None, None, None),
        P("nest", "tile", None),
    )
    out_specs = (P("nest", None, "tile", None), P(None, ("nest", "tile")))
    return jax.shard_map(shards, mesh=mesh, in_specs=in_specs, out_specs=out_specs, check_vma=False)
```

```python
import functools

import jax
import jax.numpy as jnp
from jax import lax
from jax.experimental import pallas as pl
from jax.experimental.pallas import tpu as pltpu
from jax.sharding import PartitionSpec as P

BW = 16
LANES = 128
MESH = pl.DeviceIdType.MESH
f32, bf16 = jnp.float32, jnp.bfloat16


def side_sum(x):
    zero = jnp.zeros((x.shape[0], 1), x.dtype)
    return jnp.concatenate([zero, x[:, :-1]], 1) + jnp.concatenate([x[:, 1:], zero], 1)


def kernel(
    groups, tiles, parts,
    picks, nest, parent, mix, interp, avg, land,
    x_out, p_out,
    xa, xb, xf, ws, cand, m_v, w_v, av_v, land_v, coef, strip_v, pack_v, ring_v, pool_v, tops, fb, fbs, r1, s2, r2, s3, r3, g1,
    load_sem, p_send, p_recv, h_send, h_recv, s_send, s_recv, f_send, f_recv,
):
    channels, rows, width = x_out.shape
    part = channels // parts
    slots = w_v.shape[0]
    bands = rows // 4
    n, t = lax.axis_index("nest"), lax.axis_index("tile")
    core = n + 1 - 2 * lax.rem(n, 2)
    deep = lax.rem(n + 2, groups)
    core_deep = lax.rem(core + 2, groups)
    up, down = lax.rem(t + 1, tiles), lax.rem(t + tiles - 1, tiles)
    to_up, to_down, to_core, to_deep = (n, up), (n, down), (core, t), (deep, t)
    first, last = t == 0, t == tiles - 1

    def remote(src, dst, send, recv, device):
        return pltpu.make_async_remote_copy(
            src_ref=src, dst_ref=dst, send_sem=send, recv_sem=recv, device_id=device, device_id_type=MESH
        )

    barrier = pltpu.get_barrier_semaphore()

    def greet(device):
        pl.semaphore_signal(barrier, inc=1, device_id=device, device_id_type=MESH)

    greet(to_core)
    greet(to_deep)
    pl.when(t < tiles - 1)(lambda: greet(to_up))
    pl.when(t > 0)(lambda: greet(to_down))

    def span(c):
        return pl.ds(c * part, part)

    x_loads = [pltpu.make_async_copy(nest.at[0, span(c)], x_out.at[span(c)], load_sem.at[c]) for c in range(parts)]
    own_load = pltpu.make_async_copy(parent, cand.at[3 * n + 1], load_sem.at[parts])
    mix_load = pltpu.make_async_copy(mix, m_v, load_sem.at[parts + 1])
    land_load = pltpu.make_async_copy(land.at[0], land_v, load_sem.at[parts + 2])
    w_load = pltpu.make_async_copy(interp.at[0, 0], w_v, load_sem.at[parts + 3])
    av_loads = [
        pltpu.make_async_copy(avg.at[0, 0, k], av_v.at[:, k * LANES : (k + 1) * LANES], load_sem.at[parts + 4 + k])
        for k in range(slots)
    ]
    own_load.start()
    for load in x_loads:
        load.start()
    for load in (mix_load, land_load, w_load, *av_loads):
        load.start()
    own_load.wait()

    @pl.when(first)
    def _():
        pl.semaphore_wait(barrier, 3)
        greet(to_down)

    @pl.when(t > 0)
    def _():
        pl.semaphore_wait(barrier, 4)

    pl.when(last)(lambda: greet(to_up))

    own = cand.at[3 * n + 1]
    tile_up = remote(own, cand.at[3 * n], p_send.at[0], p_recv.at[0], to_up)
    tile_down = remote(own, cand.at[3 * n + 2], p_send.at[1], p_recv.at[1], to_down)

    def to_groups(o):
        mine = cand.at[3 * n + o]
        return (
            remote(mine, mine, p_send.at[2 + o], p_recv.at[2 + o], to_core),
            remote(mine, mine, p_send.at[5 + o], p_recv.at[5 + o], to_deep),
        )

    group_copies = [to_groups(o) for o in range(3)]

    def from_below():
        tile_up.wait_recv()
        for copy in group_copies[0]:
            copy.start()

    def from_above():
        tile_down.wait_recv()
        for copy in group_copies[2]:
            copy.start()

    with jax.named_scope("own_tile"):
        tile_up.start()
        pl.when(t > 0)(tile_down.start)
        for copy in group_copies[1]:
            copy.start()

    def halos(state, step, c):
        k = (step * parts + c) * 2
        return (
            remote(state.at[rows, span(c)], state.at[0, span(c)], h_send.at[k], h_recv.at[k], to_up),
            remote(state.at[1, span(c)], state.at[rows + 1, span(c)], h_send.at[k + 1], h_recv.at[k + 1], to_down),
        )

    def halo_start(state, step, c):
        upward, downward = halos(state, step, c)
        pl.when(t < tiles - 1)(upward.start)
        pl.when(t > 0)(downward.start)

    def halo_arrived(state, step, c):
        upward, downward = halos(state, step, c)
        pl.when(t > 0)(upward.wait_recv)
        pl.when(t < tiles - 1)(downward.wait_recv)

    def halo_sent(state, step, c):
        upward, downward = halos(state, step, c)
        pl.when(t < tiles - 1)(upward.wait_send)
        pl.when(t > 0)(downward.wait_send)

    @pl.when(first)
    def _():
        ring_v[0] = jnp.zeros(ring_v.shape[1:], bf16)
        for state in (xa, xb):
            state[0] = jnp.zeros((channels, width), bf16)

    @pl.when(last)
    def _():
        ring_v[1] = jnp.zeros(ring_v.shape[1:], bf16)
        for state in (xa, xb):
            state[rows + 1] = jnp.zeros((channels, width), bf16)

    with jax.named_scope("rows_first"):
        for c in range(parts):
            x_loads[c].wait()

            def rows_first(i, carry, c=c):
                at = pl.ds(pl.multiple_of(c * part + i * 16, 16), 16)
                xa[1 : rows + 1, at, :] = jnp.swapaxes(x_out[at], 0, 1)
                return carry

            lax.fori_loop(0, part // 16, rows_first, 0)
            halo_start(xa, 0, c)

    land_load.wait()
    mix_load.wait()
    column = lax.broadcasted_iota(jnp.int32, (rows, width), 1)
    edge = jnp.minimum(column, width - 1 - column)
    ramp = jnp.maximum(BW - edge, 0).astype(f32) / BW
    factor = jnp.where(land_v[...] == 1, 0.5, 1.0)
    coef[0] = (1.0 - ramp) * (1.0 - 0.9 * factor)
    coef[1] = (1.0 - ramp) * (0.4 * factor)

    def new_value(x, above, below, sides, mixed, mine, around):
        near = above + below + jnp.asarray(0.125, bf16) * sides
        return mine * x.astype(f32) + around * (near.astype(f32) + 1.25 * mixed)

    def update(r, start, count):
        mixed = jnp.dot(m_v[start : start + count, :], xa[r + 1], preferred_element_type=f32)
        mine, around = coef[0, pl.ds(r, 1), :], coef[1, pl.ds(r, 1), :]
        for s in range(0, count, 16):
            at = slice(start + s, start + s + 16)
            x = xa[r + 1, at, :]
            y = new_value(x, xa[r, at, :], xa[r + 2, at, :], side_sum(x), mixed[s : s + 16], mine, around)
            xb[r + 1, at, :] = y.astype(bf16)

    def first_rows(begin, end):
        def body(i, carry):
            update(2 * i + 1, 0, channels)
            update(2 * i + 2, 0, channels)
            return carry

        lax.fori_loop(begin, end, body, 0)

    with jax.named_scope("first_inner"):
        first_rows(0, 2)
    with jax.named_scope("tile_on"):
        pl.when(t < tiles - 1)(from_above)
        pl.when(last)(from_below)
    with jax.named_scope("first_inner"):
        first_rows(2, (rows - 2) // 2)

    @pl.when(first)
    def _():
        pl.semaphore_wait(barrier, 1)
        tile_down.start()

    for c in range(parts):
        with jax.named_scope("first_halo_wait"):
            halo_arrived(xa, 0, c)
        with jax.named_scope("first_edges"):
            update(0, c * part, part)
            update(rows - 1, c * part, part)
        if c < parts - 1:
            halo_start(xb, 1, c)

    with jax.named_scope("tile_on"):
        pl.when(t < tiles - 1)(from_below)
        pl.when(last)(from_above)

    mid, low, high = slice(LANES, width - LANES), slice(0, LANES), slice(width - LANES, width)

    def update_mid(r, start, count):
        mixed = jnp.dot(m_v[start : start + count, :], xb[r + 1, :, mid], preferred_element_type=f32)
        mine, around = coef[0, pl.ds(r, 1), :][:, mid], coef[1, pl.ds(r, 1), :][:, mid]
        for s in range(0, count, 16):
            at = slice(start + s, start + s + 16)
            x = xb[r + 1, at, :]
            sides = side_sum(x)[:, mid]
            y = new_value(x[:, mid], xb[r, at, mid], xb[r + 2, at, mid], sides, mixed[s : s + 16], mine, around)
            xa[r + 1, at, mid] = y.astype(bf16)

    def update_out(r, start, count):
        mixed = jnp.dot(m_v[start : start + count, :], xf[r + 1], preferred_element_type=f32)
        mine, around = [
            jnp.concatenate([row[:, low], row[:, high]], axis=1) for row in (coef[0, pl.ds(r, 1), :], coef[1, pl.ds(r, 1), :])
        ]
        for s in range(0, count, 16):
            at = slice(start + s, start + s + 16)
            x = xf[r + 1, at, :]
            whole = side_sum(jnp.concatenate([x[:, :LANES], xb[r + 1, at, mid], x[:, LANES:]], axis=1))
            sides = jnp.concatenate([whole[:, low], whole[:, high]], axis=1)
            y = new_value(x, xf[r, at, :], xf[r + 2, at, :], sides, mixed[s : s + 16], mine, around)
            y = (y + ws[r, at, :]).astype(bf16)
            xa[r + 1, at, low] = y[:, :LANES]
            xa[r + 1, at, high] = y[:, LANES:]

    def inner_rows(one_row):
        def body(i, carry):
            one_row(2 * i + 1, 0, channels)
            one_row(2 * i + 2, 0, channels)
            return carry

        lax.fori_loop(0, (rows - 2) // 2, body, 0)

    for c in range(parts):
        halo_sent(xa, 0, c)
    with jax.named_scope("second_middle"):
        inner_rows(update_mid)

    w_load.wait()
    with jax.named_scope("deep_tiles_wait"):
        for o in range(3):
            group_copies[o][1].wait_recv()
    theirs = cand.at[pl.ds(3 * deep, 3)]
    onward = remote(theirs, theirs, p_send.at[8], p_recv.at[8], to_core)
    onward.start()
    with jax.named_scope("core_tiles_wait"):
        for o in range(3):
            group_copies[o][0].wait_recv()
        onward.wait_recv()
    with jax.named_scope("strip"):
        picked = jnp.concatenate([cand[picks[0, 0, k]] for k in range(slots)], axis=1)
        weights = w_v[...].reshape(slots * LANES, width)
        strip_v[...] = jnp.dot(picked, weights, preferred_element_type=f32).astype(bf16)

    cells = 2 * BW
    per = LANES // cells
    short = channels // per

    def pack(begin):
        return jnp.concatenate([strip_v[q * short : (q + 1) * short, begin : begin + cells] for q in range(per)], axis=1)

    ring_up = remote(pack_v.at[0], ring_v.at[0], s_send.at[0], s_recv.at[0], to_up)
    ring_down = remote(pack_v.at[1], ring_v.at[1], s_send.at[1], s_recv.at[1], to_down)
    with jax.named_scope("strip_send"):
        pack_v[0] = pack(width - cells)
        pack_v[1] = pack(0)
        pl.when(t < tiles - 1)(ring_up.start)
        pl.when(t > 0)(ring_down.start)
        halo_start(xb, 1, parts - 1)

    lane = lax.broadcasted_iota(jnp.int32, (1, LANES), 1)
    west_ramp = jnp.maximum(BW - lane, 0).astype(f32) / BW
    east_ramp = jnp.maximum(lane - (LANES - 1 - BW), 0).astype(f32) / BW

    def west_of(value, off):
        return pltpu.roll(value, (LANES - off) % LANES, 1) * west_ramp

    def east_of(value, off):
        return pltpu.roll(value, (2 * LANES - BW - BW - off) % LANES, 1) * east_ramp

    def spread(i, carry):
        at = pl.ds(pl.multiple_of(i * 16, 16), 16)
        for r in range(rows):
            value = strip_v[at, (r // per) * LANES : (r // per + 1) * LANES].astype(f32)
            off = (r % per) * cells
            west, east = west_of(value, off), east_of(value, off)
            ws[r, at, :LANES] = west
            ws[r, at, LANES:] = east
            xf[r + 1, at, :LANES] = (xb[r + 1, at, low].astype(f32) + west).astype(bf16)
            xf[r + 1, at, LANES:] = (xb[r + 1, at, high].astype(f32) + east).astype(bf16)
        return carry

    with jax.named_scope("strip_spread"):
        lax.fori_loop(0, channels // 16, spread, 0)

    with jax.named_scope("second_outer"):
        inner_rows(update_out)

    for load in av_loads:
        load.wait()
    pool_row = lax.broadcasted_iota(jnp.int32, (width, LANES), 0)
    pool_col = lax.broadcasted_iota(jnp.int32, (width, LANES), 1)
    pool_v[...] = jnp.where(pool_row // 4 == pool_col, 1.0 / 16.0, 0.0).astype(bf16)

    def row_total(begin, count, at):
        total = xa[begin + 1, at, :].astype(f32)
        for j in range(1, count):
            total = total + xa[begin + 1 + j, at, :].astype(f32)
        return total

    def averaged(total):
        return jnp.dot(total.astype(bf16), pool_v[...], preferred_element_type=f32).astype(bf16)

    everything = slice(0, channels)
    with jax.named_scope("feedback_inner"):
        tops[0] = row_total(1, 3, everything)
        tops[1] = row_total(rows - 4, 3, everything)
        middle = jnp.concatenate([averaged(row_total(4 * b, 4, everything)) for b in range(1, bands - 1)], axis=1)
        fb[...] = jnp.dot(middle, av_v[LANES : (bands - 1) * LANES, :], preferred_element_type=f32)

    def core_copies(c):
        return (
            remote(fbs.at[c, core], r1.at[c, 0], f_send.at[5 * c], f_recv.at[5 * c], to_core),
            remote(fbs.at[c, core_deep], r1.at[c, 1], f_send.at[5 * c + 1], f_recv.at[5 * c + 1], to_core),
        )

    def deep_copy(c):
        return remote(s2.at[c], r2.at[c], f_send.at[5 * c + 2], f_recv.at[5 * c + 2], to_deep)

    def tile_copies(c):
        return (
            remote(s3.at[c, 0], r3.at[c, 0], f_send.at[5 * c + 3], f_recv.at[5 * c + 3], to_down),
            remote(s3.at[c, 1], r3.at[c, 1], f_send.at[5 * c + 4], f_recv.at[5 * c + 4], to_up),
        )

    def stage_core(c):
        for copy in core_copies(c):
            copy.wait_recv()
        s2[c] = (fbs[c, deep].astype(f32) + r1[c, 1].astype(f32)).astype(bf16)
        deep_copy(c).start()

    def stage_deep(c):
        deep_copy(c).wait_recv()
        total = fbs[c, n].astype(f32) + r1[c, 0].astype(f32) + r2[c].astype(f32)
        s3[c, 0] = total[0].astype(bf16)
        s3[c, 1] = total[2].astype(bf16)
        g1[c] = total[1]
        for copy in tile_copies(c):
            copy.start()

    def stage_tile(c):
        for copy in tile_copies(c):
            copy.wait_recv()
        mine = cand[3 * n + 1, span(c), :].astype(f32)
        total = mine + (g1[c] + r3[c, 0].astype(f32) + r3[c, 1].astype(f32))
        p_out[span(c), :] = total.astype(bf16)

    def channels_first(c):
        def body(i, carry):
            at = pl.ds(pl.multiple_of(c * part + i * 16, 16), 16)
            x_out[at] = jnp.swapaxes(xa[1 : rows + 1, at, :], 0, 1)
            return carry

        lax.fori_loop(0, part // 16, body, 0)

    with jax.named_scope("strip_wait"):
        pl.when(t > 0)(ring_up.wait_recv)
        pl.when(t < tiles - 1)(ring_down.wait_recv)

    def halo_strip(c):
        for side, row in ((0, 0), (1, rows + 1)):
            for q in range(per):
                begin, end = max(q * short, c * part), min((q + 1) * short, (c + 1) * part)
                if begin < end:
                    at = slice(begin, end)
                    value = ring_v[side, begin - q * short : end - q * short, :].astype(f32)
                    xf[row, at, :LANES] = (xb[row, at, low].astype(f32) + west_of(value, q * cells)).astype(bf16)
                    xf[row, at, LANES:] = (xb[row, at, high].astype(f32) + east_of(value, q * cells)).astype(bf16)

    for c in range(parts):
        with jax.named_scope("second_halo_wait"):
            halo_arrived(xb, 1, c)
        with jax.named_scope("second_edges"):
            halo_strip(c)
            for r in (0, rows - 1):
                update_mid(r, c * part, part)
                update_out(r, c * part, part)
        at = slice(c * part, (c + 1) * part)
        with jax.named_scope("feedback_edges"):
            low_band = averaged(tops[0, at, :] + xa[1, at, :].astype(f32))
            high_band = averaged(tops[1, at, :] + xa[rows, at, :].astype(f32))
            terms = fb[at, :] + jnp.dot(low_band, av_v[:LANES, :], preferred_element_type=f32)
            terms = terms + jnp.dot(high_band, av_v[(bands - 1) * LANES :, :], preferred_element_type=f32)
        with jax.named_scope("feedback_slots"):
            for slot in range(3 * groups):
                total = jnp.zeros((part, LANES), f32)
                for k in range(slots):
                    total = total + (picks[0, 0, k] == slot).astype(f32) * terms[:, k * LANES : (k + 1) * LANES]
                fbs[c, slot // 3, slot % 3] = total.astype(bf16)
            for copy in core_copies(c):
                copy.start()
        if c > 0:
            with jax.named_scope("feedback_core"):
                stage_core(c - 1)
    with jax.named_scope("channels_first"):
        channels_first(0)
    with jax.named_scope("feedback_core"):
        stage_core(parts - 1)
    with jax.named_scope("channels_first"):
        for c in range(1, parts):
            channels_first(c)
    for c in range(parts):
        with jax.named_scope("feedback_deep"):
            stage_deep(c)
    for c in range(parts):
        with jax.named_scope("feedback_tile"):
            stage_tile(c)

    with jax.named_scope("sent"):
        tile_up.wait_send()
        tile_down.wait_send()
        for pair in group_copies:
            for copy in pair:
                copy.wait_send()
        onward.wait_send()
        pl.when(t < tiles - 1)(ring_up.wait_send)
        pl.when(t > 0)(ring_down.wait_send)
        for c in range(parts):
            halo_sent(xb, 1, c)
            for copy in core_copies(c):
                copy.wait_send()
            deep_copy(c).wait_send()
            for copy in tile_copies(c):
                copy.wait_send()


def write_out(x, p, nest_out, parent_out, sem):
    copies = [
        pltpu.make_async_copy(x, nest_out.at[0], sem.at[0]),
        pltpu.make_async_copy(p, parent_out, sem.at[1]),
    ]
    for copy in copies:
        copy.start()
    for copy in copies:
        copy.wait()


def shards(nest_state, parent_state, mix_weight, intersection, interp_weight, avg_weight, land_mask):
    _, channels, rows, width = nest_state.shape
    groups, tiles = lax.axis_size("nest"), lax.axis_size("tile")
    slots = intersection.shape[2]
    cells = parent_state.shape[1]
    parts = 3
    part = channels // parts
    hbm = pl.BlockSpec(memory_space=pl.ANY)
    vmem = pl.BlockSpec(memory_space=pltpu.VMEM)
    x_new, p_new = pl.pallas_call(
        functools.partial(kernel, groups, tiles, parts),
        out_shape=(pltpu.VMEM((channels, rows, width), bf16), pltpu.VMEM((channels, cells), bf16)),
        in_specs=[pl.BlockSpec(memory_space=pltpu.SMEM)] + [hbm] * 6,
        out_specs=(vmem, vmem),
        scratch_shapes=[
            pltpu.VMEM((rows + 2, channels, width), bf16),
            pltpu.VMEM((rows + 2, channels, width), bf16),
            pltpu.VMEM((rows + 2, channels, 2 * LANES), bf16),
            pltpu.VMEM((rows, channels, 2 * LANES), f32),
            pltpu.VMEM((3 * groups, channels, cells), bf16),
            pltpu.VMEM((channels, channels), bf16),
            pltpu.VMEM((slots, cells, width), bf16),
            pltpu.VMEM((width, slots * cells), bf16),
            pltpu.VMEM((rows, width), jnp.int32),
            pltpu.VMEM((2, rows, width), f32),
            pltpu.VMEM((channels, width), bf16),
            pltpu.VMEM((2, channels * 2 * BW // LANES, LANES), bf16),
            pltpu.VMEM((2, channels * 2 * BW // LANES, LANES), bf16),
            pltpu.VMEM((width, LANES), bf16),
            pltpu.VMEM((2, channels, width), f32),
            pltpu.VMEM((channels, slots * cells), f32),
            pltpu.VMEM((parts, groups, 3, part, cells), bf16),
            pltpu.VMEM((parts, 2, 3, part, cells), bf16),
            pltpu.VMEM((parts, 3, part, cells), bf16),
            pltpu.VMEM((parts, 3, part, cells), bf16),
            pltpu.VMEM((parts, 2, part, cells), bf16),
            pltpu.VMEM((parts, 2, part, cells), bf16),
            pltpu.VMEM((parts, part, cells), f32),
            pltpu.SemaphoreType.DMA((parts + 4 + slots,)),
            pltpu.SemaphoreType.DMA((9,)),
            pltpu.SemaphoreType.DMA((9,)),
            pltpu.SemaphoreType.DMA((4 * parts,)),
            pltpu.SemaphoreType.DMA((4 * parts,)),
            pltpu.SemaphoreType.DMA((2,)),
            pltpu.SemaphoreType.DMA((2,)),
            pltpu.SemaphoreType.DMA((5 * parts,)),
            pltpu.SemaphoreType.DMA((5 * parts,)),
        ],
        compiler_params=pltpu.CompilerParams(
            collective_id=0, has_side_effects=True, vmem_limit_bytes=48 * 2**20
        ),
    )(intersection, nest_state, parent_state, mix_weight, interp_weight, avg_weight, land_mask)
    return pl.pallas_call(
        write_out,
        out_shape=(
            jax.ShapeDtypeStruct(nest_state.shape, bf16),
            jax.ShapeDtypeStruct(parent_state.shape, bf16),
        ),
        in_specs=[vmem, vmem],
        out_specs=(hbm, hbm),
        scratch_shapes=[pltpu.SemaphoreType.DMA((2,))],
    )(x_new, p_new)


def solution(mesh):
    in_specs = (
        P("nest", None, "tile", None),
        P(None, ("nest", "tile")),
        P(),
        P("nest", "tile", None),
        P("nest", "tile", None, None, None),
        P("nest", "tile", None, None, None),
        P("nest", "tile", None),
    )
    out_specs = (P("nest", None, "tile", None), P(None, ("nest", "tile")))
    return jax.shard_map(shards, mesh=mesh, in_specs=in_specs, out_specs=out_specs, check_vma=False)
```

```python
import functools

import jax
import jax.numpy as jnp
from jax import lax
from jax.experimental import pallas as pl
from jax.experimental.pallas import tpu as pltpu
from jax.sharding import PartitionSpec as P

BW = 16
LANES = 128
MESH = pl.DeviceIdType.MESH
f32, bf16 = jnp.float32, jnp.bfloat16


def side_sum(x):
    zero = jnp.zeros((x.shape[0], 1), x.dtype)
    return jnp.concatenate([zero, x[:, :-1]], 1) + jnp.concatenate([x[:, 1:], zero], 1)


def kernel(
    groups, tiles, parts,
    picks, nest, parent, mix, interp, avg, land,
    x_out, p_out,
    xa, xb, xf, ws, cand, m_v, w_v, av_v, land_v, coef, strip_v, place_v, pack_v, ring_v, pool_v, tops, fb, fbs, r1, s2, r2, s3, r3, g1,
    load_sem, p_send, p_recv, h_send, h_recv, s_send, s_recv, f_send, f_recv,
):
    channels, rows, width = x_out.shape
    part = channels // parts
    slots = w_v.shape[0]
    bands = rows // 4
    n, t = lax.axis_index("nest"), lax.axis_index("tile")
    core = n + 1 - 2 * lax.rem(n, 2)
    deep = lax.rem(n + 2, groups)
    core_deep = lax.rem(core + 2, groups)
    up, down = lax.rem(t + 1, tiles), lax.rem(t + tiles - 1, tiles)
    to_up, to_down, to_core, to_deep = (n, up), (n, down), (core, t), (deep, t)
    first, last = t == 0, t == tiles - 1
    inside = jnp.logical_and(t > 0, t < tiles - 1)
    ends = jnp.logical_or(first, last)

    def remote(src, dst, send, recv, device):
        return pltpu.make_async_remote_copy(
            src_ref=src, dst_ref=dst, send_sem=send, recv_sem=recv, device_id=device, device_id_type=MESH
        )

    barrier = pltpu.get_barrier_semaphore()

    def greet(device):
        pl.semaphore_signal(barrier, inc=1, device_id=device, device_id_type=MESH)

    greet(to_core)
    greet(to_deep)
    pl.when(t < tiles - 1)(lambda: greet(to_up))
    pl.when(t > 0)(lambda: greet(to_down))

    def span(c):
        return pl.ds(c * part, part)

    x_loads = [pltpu.make_async_copy(nest.at[0, span(c)], x_out.at[span(c)], load_sem.at[c]) for c in range(parts)]
    own_load = pltpu.make_async_copy(parent, cand.at[3 * n + 1], load_sem.at[parts])
    mix_load = pltpu.make_async_copy(mix, m_v, load_sem.at[parts + 1])
    land_load = pltpu.make_async_copy(land.at[0], land_v, load_sem.at[parts + 2])
    w_load = pltpu.make_async_copy(interp.at[0, 0], w_v, load_sem.at[parts + 3])
    av_loads = [
        pltpu.make_async_copy(avg.at[0, 0, k], av_v.at[:, k * LANES : (k + 1) * LANES], load_sem.at[parts + 4 + k])
        for k in range(slots)
    ]
    own_load.start()
    for load in x_loads:
        load.start()
    for load in (mix_load, land_load, w_load, *av_loads):
        load.start()
    own_load.wait()

    @pl.when(first)
    def _():
        pl.semaphore_wait(barrier, 3)
        greet(to_down)
        greet((deep, down))

    @pl.when(inside)
    def _():
        pl.semaphore_wait(barrier, 4)

    @pl.when(last)
    def _():
        pl.semaphore_wait(barrier, 5)
        greet(to_up)
        greet((deep, up))

    own = cand.at[3 * n + 1]
    tile_up = remote(own, cand.at[3 * n], p_send.at[0], p_recv.at[0], to_up)
    tile_down = remote(own, cand.at[3 * n + 2], p_send.at[1], p_recv.at[1], to_down)

    def to_groups(o):
        mine = cand.at[3 * n + o]
        return (
            remote(mine, mine, p_send.at[2 + o], p_recv.at[2 + o], to_core),
            remote(mine, mine, p_send.at[5 + o], p_recv.at[5 + o], to_deep),
        )

    group_copies = [to_groups(o) for o in range(3)]

    over_up = remote(own, cand.at[3 * n], p_send.at[9], p_recv.at[9], (deep, up))
    over_down = remote(own, cand.at[3 * n + 2], p_send.at[9], p_recv.at[9], (deep, down))
    deep_own = cand.at[3 * deep + 1]
    beside_down = remote(deep_own, cand.at[3 * deep + 2], p_send.at[10], p_recv.at[10], to_down)
    beside_up = remote(deep_own, cand.at[3 * deep], p_send.at[10], p_recv.at[10], to_up)

    def pass_on(o):
        group_copies[o][0].start()
        pl.when(inside)(group_copies[o][1].start)

    def from_below():
        tile_up.wait_recv()
        pass_on(0)

    def from_above():
        tile_down.wait_recv()
        pass_on(2)

    with jax.named_scope("own_tile"):
        tile_up.start()
        pl.when(t > 0)(tile_down.start)
        pl.when(last)(over_up.start)
        for copy in group_copies[1]:
            copy.start()

    def halos(state, step, c):
        k = (step * parts + c) * 2
        return (
            remote(state.at[rows, span(c)], state.at[0, span(c)], h_send.at[k], h_recv.at[k], to_up),
            remote(state.at[1, span(c)], state.at[rows + 1, span(c)], h_send.at[k + 1], h_recv.at[k + 1], to_down),
        )

    def halo_start(state, step, c):
        upward, downward = halos(state, step, c)
        pl.when(t < tiles - 1)(upward.start)
        pl.when(t > 0)(downward.start)

    def halo_arrived(state, step, c):
        upward, downward = halos(state, step, c)
        pl.when(t > 0)(upward.wait_recv)
        pl.when(t < tiles - 1)(downward.wait_recv)

    def halo_sent(state, step, c):
        upward, downward = halos(state, step, c)
        pl.when(t < tiles - 1)(upward.wait_send)
        pl.when(t > 0)(downward.wait_send)

    @pl.when(first)
    def _():
        ring_v[0] = jnp.zeros(ring_v.shape[1:], bf16)
        for state in (xa, xb):
            state[0] = jnp.zeros((channels, width), bf16)

    @pl.when(last)
    def _():
        ring_v[1] = jnp.zeros(ring_v.shape[1:], bf16)
        for state in (xa, xb):
            state[rows + 1] = jnp.zeros((channels, width), bf16)

    with jax.named_scope("rows_first"):
        for c in range(parts):
            x_loads[c].wait()

            def rows_first(i, carry, c=c):
                at = pl.ds(pl.multiple_of(c * part + i * 16, 16), 16)
                xa[1 : rows + 1, at, :] = jnp.swapaxes(x_out[at], 0, 1)
                return carry

            lax.fori_loop(0, part // 16, rows_first, 0)
            halo_start(xa, 0, c)

    source = lax.broadcasted_iota(jnp.int32, (LANES, 2 * LANES), 0)
    target = lax.broadcasted_iota(jnp.int32, (LANES, 2 * LANES), 1)
    west_at = jnp.where(target < BW, target, -LANES)
    east_at = jnp.where(target >= 2 * LANES - BW, target - (2 * LANES - 2 * BW), -LANES)
    weight = jnp.where(target < BW, BW - target, target - (2 * LANES - BW - 1)).astype(f32) / BW
    for j in range(LANES // (2 * BW)):
        here = source - j * 2 * BW
        place_v[j] = jnp.where((here == west_at) | (here == east_at), weight, 0.0).astype(bf16)

    land_load.wait()
    mix_load.wait()
    column = lax.broadcasted_iota(jnp.int32, (rows, width), 1)
    edge = jnp.minimum(column, width - 1 - column)
    ramp = jnp.maximum(BW - edge, 0).astype(f32) / BW
    factor = jnp.where(land_v[...] == 1, 0.5, 1.0)
    coef[0] = (1.0 - ramp) * (1.0 - 0.9 * factor)
    coef[1] = (1.0 - ramp) * (0.4 * factor)

    def new_value(x, above, below, sides, mixed, mine, around):
        near = above + below + jnp.asarray(0.125, bf16) * sides
        return mine * x.astype(f32) + around * (near.astype(f32) + 1.25 * mixed)

    def update(r, start, count):
        mixed = jnp.dot(m_v[start : start + count, :], xa[r + 1], preferred_element_type=f32)
        mine, around = coef[0, pl.ds(r, 1), :], coef[1, pl.ds(r, 1), :]
        for s in range(0, count, 16):
            at = slice(start + s, start + s + 16)
            x = xa[r + 1, at, :]
            y = new_value(x, xa[r, at, :], xa[r + 2, at, :], side_sum(x), mixed[s : s + 16], mine, around)
            xb[r + 1, at, :] = y.astype(bf16)

    def first_rows(begin, end):
        def body(i, carry):
            update(2 * i + 1, 0, channels)
            update(2 * i + 2, 0, channels)
            return carry

        lax.fori_loop(begin, end, body, 0)

    with jax.named_scope("first_inner"):
        first_rows(0, (rows - 2) // 2)
    with jax.named_scope("tile_on"):
        pl.when(t < tiles - 1)(from_above)
        pl.when(t > 0)(from_below)
        group_copies[1][1].wait_recv()
        pl.when(t == 1)(beside_down.start)
        pl.when(t == tiles - 2)(beside_up.start)

    mid, low, high = slice(LANES, width - LANES), slice(0, LANES), slice(width - LANES, width)

    def update_mid(r, start, count):
        mixed = jnp.dot(m_v[start : start + count, :], xb[r + 1, :, mid], preferred_element_type=f32)
        mine, around = coef[0, pl.ds(r, 1), :][:, mid], coef[1, pl.ds(r, 1), :][:, mid]
        for s in range(0, count, 16):
            at = slice(start + s, start + s + 16)
            x = xb[r + 1, at, :]
            sides = side_sum(x)[:, mid]
            y = new_value(x[:, mid], xb[r, at, mid], xb[r + 2, at, mid], sides, mixed[s : s + 16], mine, around)
            xa[r + 1, at, mid] = y.astype(bf16)

    def update_out(r, start, count):
        mixed = jnp.dot(m_v[start : start + count, :], xf[r + 1], preferred_element_type=f32)
        mine, around = [
            jnp.concatenate([row[:, low], row[:, high]], axis=1) for row in (coef[0, pl.ds(r, 1), :], coef[1, pl.ds(r, 1), :])
        ]
        for s in range(0, count, 16):
            at = slice(start + s, start + s + 16)
            x = xf[r + 1, at, :]
            whole = side_sum(jnp.concatenate([x[:, :LANES], xb[r + 1, at, mid], x[:, LANES:]], axis=1))
            sides = jnp.concatenate([whole[:, low], whole[:, high]], axis=1)
            y = new_value(x, xf[r, at, :], xf[r + 2, at, :], sides, mixed[s : s + 16], mine, around)
            y = (y + ws[r, at, :].astype(f32)).astype(bf16)
            xa[r + 1, at, low] = y[:, :LANES]
            xa[r + 1, at, high] = y[:, LANES:]

    def pairs(one_row, begin, end):
        def body(i, carry):
            one_row(2 * i, 0, channels)
            one_row(2 * i + 1, 0, channels)
            return carry

        lax.fori_loop(begin // 2, end // 2, body, 0)

    stops = [2 + 2 * ((rows - 4) // 2 * c // parts) for c in range(parts + 1)]
    for c in range(parts):
        with jax.named_scope("first_halo_wait"):
            halo_arrived(xa, 0, c)
        with jax.named_scope("first_edges"):
            update(0, c * part, part)
            update(rows - 1, c * part, part)
        if c < parts - 1:
            halo_start(xb, 1, c)
            with jax.named_scope("second_middle"):
                pairs(update_mid, stops[c], stops[c + 1])
        if c == 1:

            @pl.when(first)
            def _():
                pl.semaphore_wait(barrier, 2)
                tile_down.start()
                over_down.start()

    with jax.named_scope("tile_on"):
        pl.when(first)(from_below)
        pl.when(last)(from_above)
    with jax.named_scope("second_middle"):
        pairs(update_mid, stops[parts - 1], stops[parts])
        update_mid(1, 0, channels)
        update_mid(rows - 2, 0, channels)

    w_load.wait()
    with jax.named_scope("deep_tiles_wait"):

        @pl.when(inside)
        def _():
            group_copies[0][1].wait_recv()
            group_copies[2][1].wait_recv()

        @pl.when(first)
        def _():
            over_up.wait_recv()
            beside_down.wait_recv()

        @pl.when(last)
        def _():
            over_down.wait_recv()
            beside_up.wait_recv()

    theirs = cand.at[pl.ds(3 * deep, 3)]
    onward = remote(theirs, theirs, p_send.at[8], p_recv.at[8], to_core)
    onward.start()
    with jax.named_scope("core_tiles_wait"):
        for o in range(3):
            group_copies[o][0].wait_recv()
        onward.wait_recv()
    with jax.named_scope("strip"):
        picked = jnp.concatenate([cand[picks[0, 0, k]] for k in range(slots)], axis=1)
        weights = w_v[...].reshape(slots * LANES, width)
        strip_v[...] = jnp.dot(picked, weights, preferred_element_type=f32).astype(bf16)

    cells = 2 * BW
    per = LANES // cells
    short = channels // per

    def pack(begin):
        return jnp.concatenate([strip_v[q * short : (q + 1) * short, begin : begin + cells] for q in range(per)], axis=1)

    ring_up = remote(pack_v.at[0], ring_v.at[0], s_send.at[0], s_recv.at[0], to_up)
    ring_down = remote(pack_v.at[1], ring_v.at[1], s_send.at[1], s_recv.at[1], to_down)
    with jax.named_scope("strip_send"):
        pack_v[0] = pack(width - cells)
        pack_v[1] = pack(0)
        pl.when(t < tiles - 1)(ring_up.start)
        pl.when(t > 0)(ring_down.start)
        halo_start(xb, 1, parts - 1)

    def placed(value, j):
        return jnp.dot(value, place_v[j], preferred_element_type=f32)

    def fixed(row, at, wide):
        xf[row, at, :LANES] = (xb[row, at, low].astype(f32) + wide[:, :LANES]).astype(bf16)
        xf[row, at, LANES:] = (xb[row, at, high].astype(f32) + wide[:, LANES:]).astype(bf16)

    def spread(b, carry):
        value = strip_v[:, pl.ds(pl.multiple_of(b * LANES, LANES), LANES)]
        for j in range(per):
            wide = placed(value, j)
            ws[per * b + j] = wide.astype(bf16)
            fixed(per * b + j + 1, slice(0, channels), wide)
        return carry

    with jax.named_scope("strip_spread"):
        lax.fori_loop(0, rows // per, spread, 0)

    with jax.named_scope("second_outer"):
        update_out(1, 0, channels)
        update_out(rows - 2, 0, channels)
        pairs(update_out, 2, rows - 2)

    for load in av_loads:
        load.wait()
    pool_row = lax.broadcasted_iota(jnp.int32, (width, LANES), 0)
    pool_col = lax.broadcasted_iota(jnp.int32, (width, LANES), 1)
    pool_v[...] = jnp.where(pool_row // 4 == pool_col, 1.0 / 16.0, 0.0).astype(bf16)

    def row_total(begin, count, at):
        total = xa[begin + 1, at, :].astype(f32)
        for j in range(1, count):
            total = total + xa[begin + 1 + j, at, :].astype(f32)
        return total

    def averaged(total):
        return jnp.dot(total.astype(bf16), pool_v[...], preferred_element_type=f32).astype(bf16)

    everything = slice(0, channels)
    with jax.named_scope("feedback_inner"):
        tops[0] = row_total(1, 3, everything)
        tops[1] = row_total(rows - 4, 3, everything)
        middle = jnp.concatenate([averaged(row_total(4 * b, 4, everything)) for b in range(1, bands - 1)], axis=1)
        fb[...] = jnp.dot(middle, av_v[LANES : (bands - 1) * LANES, :], preferred_element_type=f32)

    def core_copies(c):
        return (
            remote(fbs.at[c, core], r1.at[c, 0], f_send.at[5 * c], f_recv.at[5 * c], to_core),
            remote(fbs.at[c, core_deep], r1.at[c, 1], f_send.at[5 * c + 1], f_recv.at[5 * c + 1], to_core),
        )

    def deep_copy(c):
        return remote(s2.at[c], r2.at[c], f_send.at[5 * c + 2], f_recv.at[5 * c + 2], to_deep)

    def tile_copies(c):
        return (
            remote(s3.at[c, 0], r3.at[c, 0], f_send.at[5 * c + 3], f_recv.at[5 * c + 3], to_down),
            remote(s3.at[c, 1], r3.at[c, 1], f_send.at[5 * c + 4], f_recv.at[5 * c + 4], to_up),
        )

    def stage_core(c):
        for copy in core_copies(c):
            copy.wait_recv()
        s2[c] = (fbs[c, deep].astype(f32) + r1[c, 1].astype(f32)).astype(bf16)
        deep_copy(c).start()

    def stage_deep(c):
        deep_copy(c).wait_recv()
        total = fbs[c, n].astype(f32) + r1[c, 0].astype(f32) + r2[c].astype(f32)
        s3[c, 0] = total[0].astype(bf16)
        s3[c, 1] = total[2].astype(bf16)
        g1[c] = total[1]
        for copy in tile_copies(c):
            copy.start()

    def stage_tile(c):
        for copy in tile_copies(c):
            copy.wait_recv()
        mine = cand[3 * n + 1, span(c), :].astype(f32)
        total = mine + (g1[c] + r3[c, 0].astype(f32) + r3[c, 1].astype(f32))
        p_out[span(c), :] = total.astype(bf16)

    def channels_first(c):
        def body(i, carry):
            at = pl.ds(pl.multiple_of(c * part + i * 16, 16), 16)
            x_out[at] = jnp.swapaxes(xa[1 : rows + 1, at, :], 0, 1)
            return carry

        lax.fori_loop(0, part // 16, body, 0)

    with jax.named_scope("strip_wait"):
        pl.when(t > 0)(ring_up.wait_recv)
        pl.when(t < tiles - 1)(ring_down.wait_recv)

    def halo_strip(c):
        for side, row in ((0, 0), (1, rows + 1)):
            for q in range(per):
                begin, end = max(q * short, c * part), min((q + 1) * short, (c + 1) * part)
                if begin < end:
                    at = slice(begin, end)
                    fixed(row, at, placed(ring_v[side, begin - q * short : end - q * short, :], q))

    for c in range(parts):
        halo_sent(xa, 0, c)
    for c in range(parts):
        with jax.named_scope("second_halo_wait"):
            halo_arrived(xb, 1, c)
        with jax.named_scope("second_edges"):
            halo_strip(c)
            for r in (0, rows - 1):
                update_mid(r, c * part, part)
                update_out(r, c * part, part)
        at = slice(c * part, (c + 1) * part)
        with jax.named_scope("feedback_edges"):
            low_band = averaged(tops[0, at, :] + xa[1, at, :].astype(f32))
            high_band = averaged(tops[1, at, :] + xa[rows, at, :].astype(f32))
            terms = fb[at, :] + jnp.dot(low_band, av_v[:LANES, :], preferred_element_type=f32)
            terms = terms + jnp.dot(high_band, av_v[(bands - 1) * LANES :, :], preferred_element_type=f32)
        with jax.named_scope("feedback_slots"):
            for slot in range(3 * groups):
                total = jnp.zeros((part, LANES), f32)
                for k in range(slots):
                    total = total + (picks[0, 0, k] == slot).astype(f32) * terms[:, k * LANES : (k + 1) * LANES]
                fbs[c, slot // 3, slot % 3] = total.astype(bf16)
            for copy in core_copies(c):
                copy.start()
        if c > 0:
            with jax.named_scope("feedback_core"):
                stage_core(c - 1)
    with jax.named_scope("channels_first"):
        channels_first(0)
    with jax.named_scope("feedback_core"):
        stage_core(parts - 1)
    with jax.named_scope("channels_first"):
        for c in range(1, parts):
            channels_first(c)
    for c in range(parts):
        with jax.named_scope("feedback_deep"):
            stage_deep(c)
    for c in range(parts):
        with jax.named_scope("feedback_tile"):
            stage_tile(c)

    with jax.named_scope("sent"):
        tile_up.wait_send()
        tile_down.wait_send()
        for copy, _ in group_copies:
            copy.wait_send()
        group_copies[1][1].wait_send()

        @pl.when(inside)
        def _():
            group_copies[0][1].wait_send()
            group_copies[2][1].wait_send()

        pl.when(ends)(over_up.wait_send)
        pl.when(jnp.logical_or(t == 1, t == tiles - 2))(beside_up.wait_send)
        onward.wait_send()
        pl.when(t < tiles - 1)(ring_up.wait_send)
        pl.when(t > 0)(ring_down.wait_send)
        for c in range(parts):
            halo_sent(xb, 1, c)
            for copy in core_copies(c):
                copy.wait_send()
            deep_copy(c).wait_send()
            for copy in tile_copies(c):
                copy.wait_send()


def write_out(pieces, x, p, nest_out, parent_out, sem):
    size = x.shape[0] // pieces
    copies = [pltpu.make_async_copy(p, parent_out, sem.at[pieces])]
    for c in range(pieces):
        at = pl.ds(c * size, size)
        copies.append(pltpu.make_async_copy(x.at[at], nest_out.at[0, at], sem.at[c]))
    for copy in copies:
        copy.start()
    for copy in copies:
        copy.wait()


def shards(nest_state, parent_state, mix_weight, intersection, interp_weight, avg_weight, land_mask):
    _, channels, rows, width = nest_state.shape
    groups, tiles = lax.axis_size("nest"), lax.axis_size("tile")
    slots = intersection.shape[2]
    cells = parent_state.shape[1]
    parts = 3
    part = channels // parts
    hbm = pl.BlockSpec(memory_space=pl.ANY)
    vmem = pl.BlockSpec(memory_space=pltpu.VMEM)
    x_new, p_new = pl.pallas_call(
        functools.partial(kernel, groups, tiles, parts),
        out_shape=(pltpu.VMEM((channels, rows, width), bf16), pltpu.VMEM((channels, cells), bf16)),
        in_specs=[pl.BlockSpec(memory_space=pltpu.SMEM)] + [hbm] * 6,
        out_specs=(vmem, vmem),
        scratch_shapes=[
            pltpu.VMEM((rows + 2, channels, width), bf16),
            pltpu.VMEM((rows + 2, channels, width), bf16),
            pltpu.VMEM((rows + 2, channels, 2 * LANES), bf16),
            pltpu.VMEM((rows, channels, 2 * LANES), bf16),
            pltpu.VMEM((3 * groups, channels, cells), bf16),
            pltpu.VMEM((channels, channels), bf16),
            pltpu.VMEM((slots, cells, width), bf16),
            pltpu.VMEM((width, slots * cells), bf16),
            pltpu.VMEM((rows, width), jnp.int32),
            pltpu.VMEM((2, rows, width), f32),
            pltpu.VMEM((channels, width), bf16),
            pltpu.VMEM((LANES // (2 * BW), LANES, 2 * LANES), bf16),
            pltpu.VMEM((2, channels * 2 * BW // LANES, LANES), bf16),
            pltpu.VMEM((2, channels * 2 * BW // LANES, LANES), bf16),
            pltpu.VMEM((width, LANES), bf16),
            pltpu.VMEM((2, channels, width), f32),
            pltpu.VMEM((channels, slots * cells), f32),
            pltpu.VMEM((parts, groups, 3, part, cells), bf16),
            pltpu.VMEM((parts, 2, 3, part, cells), bf16),
            pltpu.VMEM((parts, 3, part, cells), bf16),
            pltpu.VMEM((parts, 3, part, cells), bf16),
            pltpu.VMEM((parts, 2, part, cells), bf16),
            pltpu.VMEM((parts, 2, part, cells), bf16),
            pltpu.VMEM((parts, part, cells), f32),
            pltpu.SemaphoreType.DMA((parts + 4 + slots,)),
            pltpu.SemaphoreType.DMA((11,)),
            pltpu.SemaphoreType.DMA((11,)),
            pltpu.SemaphoreType.DMA((4 * parts,)),
            pltpu.SemaphoreType.DMA((4 * parts,)),
            pltpu.SemaphoreType.DMA((2,)),
            pltpu.SemaphoreType.DMA((2,)),
            pltpu.SemaphoreType.DMA((5 * parts,)),
            pltpu.SemaphoreType.DMA((5 * parts,)),
        ],
        compiler_params=pltpu.CompilerParams(
            collective_id=0, has_side_effects=True, vmem_limit_bytes=48 * 2**20
        ),
    )(intersection, nest_state, parent_state, mix_weight, interp_weight, avg_weight, land_mask)
    return pl.pallas_call(
        functools.partial(write_out, 8),
        out_shape=(
            jax.ShapeDtypeStruct(nest_state.shape, bf16),
            jax.ShapeDtypeStruct(parent_state.shape, bf16),
        ),
        in_specs=[hbm, hbm],
        out_specs=(hbm, hbm),
        scratch_shapes=[pltpu.SemaphoreType.DMA((9,))],
        compiler_params=pltpu.CompilerParams(vmem_limit_bytes=8 * 2**20),
    )(x_new, p_new)


def solution(mesh):
    in_specs = (
        P("nest", None, "tile", None),
        P(None, ("nest", "tile")),
        P(),
        P("nest", "tile", None),
        P("nest", "tile", None, None, None),
        P("nest", "tile", None, None, None),
        P("nest", "tile", None),
    )
    out_specs = (P("nest", None, "tile", None), P(None, ("nest", "tile")))
    return jax.shard_map(shards, mesh=mesh, in_specs=in_specs, out_specs=out_specs, check_vma=False)
```

```python
import functools

import jax
import jax.numpy as jnp
from jax import lax
from jax.experimental import pallas as pl
from jax.experimental.pallas import tpu as pltpu
from jax.sharding import PartitionSpec as P

BW = 16
LANES = 128
SIDE = 4
MESH = pl.DeviceIdType.MESH
f32, bf16 = jnp.float32, jnp.bfloat16


def side_sum(x):
    zero = jnp.zeros((x.shape[0], 1), x.dtype)
    return jnp.concatenate([zero, x[:, :-1]], 1) + jnp.concatenate([x[:, 1:], zero], 1)


def kernel(
    groups, tiles, parts,
    picks, nest, parent, mix, interp, avg, land,
    x_out, p_out,
    xa, xb, xf, ws, cand, m_v, w_v, av_v, land_v, coef, strip_v, place_v, pack_v, ring_v, pool_v, tops, fb, fbs, r1, s2, r2, s3, r3, g1,
    load_sem, p_send, p_recv, h_send, h_recv, s_send, s_recv, f_send, f_recv,
):
    channels, rows, width = x_out.shape
    part = channels // parts
    slots = w_v.shape[0]
    bands = rows // 4
    n, t = lax.axis_index("nest"), lax.axis_index("tile")
    core = n + 1 - 2 * lax.rem(n, 2)
    deep = lax.rem(n + 2, groups)
    core_deep = lax.rem(core + 2, groups)
    up, down = lax.rem(t + 1, tiles), lax.rem(t + tiles - 1, tiles)
    to_up, to_down, to_core, to_deep = (n, up), (n, down), (core, t), (deep, t)
    first, last = t == 0, t == tiles - 1
    inside = jnp.logical_and(t > 0, t < tiles - 1)
    ends = jnp.logical_or(first, last)

    def remote(src, dst, send, recv, device):
        return pltpu.make_async_remote_copy(
            src_ref=src, dst_ref=dst, send_sem=send, recv_sem=recv, device_id=device, device_id_type=MESH
        )

    barrier = pltpu.get_barrier_semaphore()

    def greet(device):
        pl.semaphore_signal(barrier, inc=1, device_id=device, device_id_type=MESH)

    greet(to_core)
    greet(to_deep)
    pl.when(t < tiles - 1)(lambda: greet(to_up))
    pl.when(t > 0)(lambda: greet(to_down))

    def span(c):
        return pl.ds(c * part, part)

    x_loads = [pltpu.make_async_copy(nest.at[0, span(c)], x_out.at[span(c)], load_sem.at[c]) for c in range(parts)]
    own_load = pltpu.make_async_copy(parent, cand.at[3 * n + 1], load_sem.at[parts])
    mix_load = pltpu.make_async_copy(mix, m_v, load_sem.at[parts + 1])
    land_load = pltpu.make_async_copy(land.at[0], land_v, load_sem.at[parts + 2])
    w_load = pltpu.make_async_copy(interp.at[0, 0], w_v, load_sem.at[parts + 3])
    av_loads = [
        pltpu.make_async_copy(avg.at[0, 0, k], av_v.at[:, k * LANES : (k + 1) * LANES], load_sem.at[parts + 4 + k])
        for k in range(slots)
    ]
    own_load.start()
    for load in x_loads:
        load.start()
    for load in (mix_load, land_load, w_load, *av_loads):
        load.start()
    def rows_first(c):
        x_loads[c].wait()

        def body(i, carry):
            at = pl.ds(pl.multiple_of(c * part + i * 16, 16), 16)
            xa[1 : rows + 1, at, :] = jnp.swapaxes(x_out[at], 0, 1)
            return carry

        lax.fori_loop(0, part // 16, body, 0)

    @pl.when(first)
    def _():
        pl.semaphore_wait(barrier, 3)
        greet(to_down)
        greet((deep, down))

    @pl.when(inside)
    def _():
        pl.semaphore_wait(barrier, 4)

    @pl.when(last)
    def _():
        pl.semaphore_wait(barrier, 5)
        greet(to_up)
        greet((deep, up))

    own_load.wait()
    own = cand.at[3 * n + 1]
    tile_up = remote(own, cand.at[3 * n], p_send.at[0], p_recv.at[0], to_up)
    tile_down = remote(own, cand.at[3 * n + 2], p_send.at[1], p_recv.at[1], to_down)

    def to_groups(o):
        mine = cand.at[3 * n + o]
        return (
            remote(mine, mine, p_send.at[2 + o], p_recv.at[2 + o], to_core),
            remote(mine, mine, p_send.at[5 + o], p_recv.at[5 + o], to_deep),
        )

    group_copies = [to_groups(o) for o in range(3)]

    over_up = remote(own, cand.at[3 * n], p_send.at[9], p_recv.at[9], (deep, up))
    over_down = remote(own, cand.at[3 * n + 2], p_send.at[9], p_recv.at[9], (deep, down))
    def beside(k, source, target, device):
        return remote(cand.at[3 * deep + source], cand.at[3 * deep + target], p_send.at[10 + k], p_recv.at[10 + k], device)

    beside_down = beside(0, 1, 2, to_down), beside(1, 0, 1, to_down)
    beside_up = beside(0, 1, 0, to_up), beside(1, 2, 1, to_up)
    after_first, before_last = t == 1, t == tiles - 2

    def pass_on(o):
        group_copies[o][0].start()
        pl.when(inside)(group_copies[o][1].start)

    def from_below():
        tile_up.wait_recv()
        pass_on(0)

    def from_above():
        tile_down.wait_recv()
        pass_on(2)

    with jax.named_scope("own_tile"):
        tile_up.start()
        pl.when(t > 0)(tile_down.start)
        pl.when(last)(over_up.start)
        pass_on(1)

    def halos(state, step, c):
        k = (step * parts + c) * 2
        return (
            remote(state.at[rows, span(c)], state.at[0, span(c)], h_send.at[k], h_recv.at[k], to_up),
            remote(state.at[1, span(c)], state.at[rows + 1, span(c)], h_send.at[k + 1], h_recv.at[k + 1], to_down),
        )

    def halo_start(state, step, c):
        upward, downward = halos(state, step, c)
        pl.when(t < tiles - 1)(upward.start)
        pl.when(t > 0)(downward.start)

    def halo_arrived(state, step, c):
        upward, downward = halos(state, step, c)
        pl.when(t > 0)(upward.wait_recv)
        pl.when(t < tiles - 1)(downward.wait_recv)

    def halo_sent(state, step, c):
        upward, downward = halos(state, step, c)
        pl.when(t < tiles - 1)(upward.wait_send)
        pl.when(t > 0)(downward.wait_send)

    @pl.when(first)
    def _():
        ring_v[0] = jnp.zeros(ring_v.shape[1:], bf16)
        for state in (xa, xb):
            state[0] = jnp.zeros((channels, width), bf16)

    @pl.when(last)
    def _():
        ring_v[1] = jnp.zeros(ring_v.shape[1:], bf16)
        for state in (xa, xb):
            state[rows + 1] = jnp.zeros((channels, width), bf16)

    with jax.named_scope("rows_first"):
        for c in range(parts):
            rows_first(c)
            halo_start(xa, 0, c)

    source = lax.broadcasted_iota(jnp.int32, (LANES, 2 * LANES), 0)
    target = lax.broadcasted_iota(jnp.int32, (LANES, 2 * LANES), 1)
    west_at = jnp.where(target < BW, target, -LANES)
    east_at = jnp.where(target >= 2 * LANES - BW, target - (2 * LANES - 2 * BW), -LANES)
    weight = jnp.where(target < BW, BW - target, target - (2 * LANES - BW - 1)).astype(f32) / BW
    for j in range(LANES // (2 * BW)):
        here = source - j * 2 * BW
        place_v[j] = jnp.where((here == west_at) | (here == east_at), weight, 0.0).astype(bf16)

    land_load.wait()
    mix_load.wait()
    column = lax.broadcasted_iota(jnp.int32, (rows, width), 1)
    edge = jnp.minimum(column, width - 1 - column)
    ramp = jnp.maximum(BW - edge, 0).astype(f32) / BW
    factor = jnp.where(land_v[...] == 1, 0.5, 1.0)
    coef[0] = (1.0 - ramp) * (1.0 - 0.9 * factor)
    coef[1] = (1.0 - ramp) * (0.4 * factor)

    def new_value(x, above, below, sides, mixed, mine, around):
        near = above + below + jnp.asarray(0.125, bf16) * sides
        return mine * x.astype(f32) + around * (near.astype(f32) + 1.25 * mixed)

    def update(r, start, count):
        mixed = jnp.dot(m_v[start : start + count, :], xa[r + 1], preferred_element_type=f32)
        mine, around = coef[0, pl.ds(r, 1), :], coef[1, pl.ds(r, 1), :]
        for s in range(0, count, 16):
            at = slice(start + s, start + s + 16)
            x = xa[r + 1, at, :]
            y = new_value(x, xa[r, at, :], xa[r + 2, at, :], side_sum(x), mixed[s : s + 16], mine, around)
            xb[r + 1, at, :] = y.astype(bf16)

    def first_rows(begin, end):
        def body(i, carry):
            update(2 * i + 1, 0, channels)
            update(2 * i + 2, 0, channels)
            return carry

        lax.fori_loop(begin, end, body, 0)

    row_start, row_end = lax.rem(t, SIDE) == 0, lax.rem(t, SIDE) == SIDE - 1
    with jax.named_scope("first_inner"):
        first_rows(0, 3)
    with jax.named_scope("tile_on"):
        pl.when(after_first)(from_below)
        pl.when(jnp.logical_not(row_end))(from_above)
        pl.when(jnp.logical_not(jnp.logical_or(row_start, after_first)))(from_below)

        @pl.when(jnp.logical_or(after_first, before_last))
        def _():
            group_copies[1][1].wait_recv()

        pl.when(after_first)(beside_down[0].start)
        pl.when(before_last)(beside_up[0].start)
    with jax.named_scope("first_inner"):
        first_rows(3, (rows - 2) // 2)

    mid, low, high = slice(LANES, width - LANES), slice(0, LANES), slice(width - LANES, width)

    def update_mid(r, start, count):
        mixed = jnp.dot(m_v[start : start + count, :], xb[r + 1, :, mid], preferred_element_type=f32)
        mine, around = coef[0, pl.ds(r, 1), :][:, mid], coef[1, pl.ds(r, 1), :][:, mid]
        for s in range(0, count, 16):
            at = slice(start + s, start + s + 16)
            x = xb[r + 1, at, :]
            sides = side_sum(x)[:, mid]
            y = new_value(x[:, mid], xb[r, at, mid], xb[r + 2, at, mid], sides, mixed[s : s + 16], mine, around)
            xa[r + 1, at, mid] = y.astype(bf16)

    def update_out(r, start, count):
        mixed = jnp.dot(m_v[start : start + count, :], xf[r + 1], preferred_element_type=f32)
        mine, around = [
            jnp.concatenate([row[:, low], row[:, high]], axis=1) for row in (coef[0, pl.ds(r, 1), :], coef[1, pl.ds(r, 1), :])
        ]
        for s in range(0, count, 16):
            at = slice(start + s, start + s + 16)
            x = xf[r + 1, at, :]
            whole = side_sum(jnp.concatenate([x[:, :LANES], xb[r + 1, at, mid], x[:, LANES:]], axis=1))
            sides = jnp.concatenate([whole[:, low], whole[:, high]], axis=1)
            y = new_value(x, xf[r, at, :], xf[r + 2, at, :], sides, mixed[s : s + 16], mine, around)
            y = (y + ws[r, at, :].astype(f32)).astype(bf16)
            xa[r + 1, at, low] = y[:, :LANES]
            xa[r + 1, at, high] = y[:, LANES:]

    def quads(one_row, begin, end):
        def body(i, carry):
            for j in range(4):
                one_row(begin + 4 * i + j, 0, channels)
            return carry

        lax.fori_loop(0, (end - begin) // 4, body, 0)

    theirs = cand.at[pl.ds(3 * deep, 3)]
    onward = remote(theirs, theirs, p_send.at[8], p_recv.at[8], to_core)

    stops = (2, 6, rows - 2)
    for c in range(parts):
        if c == parts - 1:
            with jax.named_scope("deep_tiles_wait"):

                @pl.when(inside)
                def _():
                    pl.when(jnp.logical_not(after_first))(group_copies[0][1].wait_recv)
                    pl.when(jnp.logical_not(before_last))(group_copies[2][1].wait_recv)

                    @pl.when(jnp.logical_not(jnp.logical_or(after_first, before_last)))
                    def _():
                        group_copies[1][1].wait_recv()

                    onward.start()

        with jax.named_scope("first_halo_wait"):
            halo_arrived(xa, 0, c)
        with jax.named_scope("first_edges"):
            update(0, c * part, part)
            update(rows - 1, c * part, part)
        if c == 0:
            with jax.named_scope("tile_on"):

                @pl.when(after_first)
                def _():
                    group_copies[0][1].wait_recv()
                    beside_down[1].start()

                @pl.when(before_last)
                def _():
                    group_copies[2][1].wait_recv()
                    beside_up[1].start()

        if c < parts - 1:
            halo_start(xb, 1, c)
        if c == 0:
            with jax.named_scope("tile_on"):
                pl.when(jnp.logical_and(row_end, t < tiles - 1))(from_above)
                pl.when(jnp.logical_and(row_start, t > 0))(from_below)
        if c < parts - 1:
            with jax.named_scope("second_middle"):
                quads(update_mid, stops[c], stops[c + 1])
        if c == 1:

            @pl.when(first)
            def _():
                pl.semaphore_wait(barrier, 2)
                tile_down.start()
                over_down.start()

    with jax.named_scope("tile_on"):
        pl.when(first)(from_below)
        pl.when(last)(from_above)
    with jax.named_scope("second_middle"):
        update_mid(1, 0, channels)
        update_mid(rows - 2, 0, channels)

    w_load.wait()
    with jax.named_scope("deep_tiles_wait"):

        @pl.when(first)
        def _():
            over_up.wait_recv()
            beside_down[0].wait_recv()
            beside_down[1].wait_recv()

        @pl.when(last)
        def _():
            over_down.wait_recv()
            beside_up[0].wait_recv()
            beside_up[1].wait_recv()

        pl.when(ends)(onward.start)
    with jax.named_scope("core_tiles_wait"):
        for o in range(3):
            group_copies[o][0].wait_recv()
        onward.wait_recv()
    with jax.named_scope("strip"):
        picked = jnp.concatenate([cand[picks[0, 0, k]] for k in range(slots)], axis=1)
        weights = w_v[...].reshape(slots * LANES, width)
        strip_v[...] = jnp.dot(picked, weights, preferred_element_type=f32).astype(bf16)

    cells = 2 * BW
    per = LANES // cells
    short = channels // per

    def pack(begin):
        return jnp.concatenate([strip_v[q * short : (q + 1) * short, begin : begin + cells] for q in range(per)], axis=1)

    ring_up = remote(pack_v.at[0], ring_v.at[0], s_send.at[0], s_recv.at[0], to_up)
    ring_down = remote(pack_v.at[1], ring_v.at[1], s_send.at[1], s_recv.at[1], to_down)
    with jax.named_scope("strip_send"):
        pack_v[0] = pack(width - cells)
        pack_v[1] = pack(0)
        pl.when(t < tiles - 1)(ring_up.start)
        pl.when(t > 0)(ring_down.start)
        halo_start(xb, 1, parts - 1)

    def placed(value, j):
        return jnp.dot(value, place_v[j], preferred_element_type=f32)

    def fixed(row, at, wide):
        xf[row, at, :LANES] = (xb[row, at, low].astype(f32) + wide[:, :LANES]).astype(bf16)
        xf[row, at, LANES:] = (xb[row, at, high].astype(f32) + wide[:, LANES:]).astype(bf16)

    def spread(j, carry):
        value = jnp.concatenate([strip_v[:, b * LANES : (b + 1) * LANES] for b in range(rows // per)], axis=0)
        wide = placed(value, j)
        for b in range(rows // per):
            block = wide[b * channels : (b + 1) * channels]
            ws[per * b + j] = block.astype(bf16)
            fixed(per * b + j + 1, slice(0, channels), block)
        return carry

    with jax.named_scope("strip_spread"):
        lax.fori_loop(0, per, spread, 0)

    with jax.named_scope("second_outer"):
        update_out(1, 0, channels)
        update_out(rows - 2, 0, channels)
        quads(update_out, 2, rows - 2)

    for load in av_loads:
        load.wait()
    pool_row = lax.broadcasted_iota(jnp.int32, (width, LANES), 0)
    pool_col = lax.broadcasted_iota(jnp.int32, (width, LANES), 1)
    pool_v[...] = jnp.where(pool_row // 4 == pool_col, 1.0 / 16.0, 0.0).astype(bf16)

    def row_total(begin, count, at):
        total = xa[begin + 1, at, :].astype(f32)
        for j in range(1, count):
            total = total + xa[begin + 1 + j, at, :].astype(f32)
        return total

    def averaged(total):
        return jnp.dot(total.astype(bf16), pool_v[...], preferred_element_type=f32).astype(bf16)

    everything = slice(0, channels)
    with jax.named_scope("feedback_inner"):
        tops[0] = row_total(1, 3, everything)
        tops[1] = row_total(rows - 4, 3, everything)
        middle = jnp.concatenate([averaged(row_total(4 * b, 4, everything)) for b in range(1, bands - 1)], axis=1)
        fb[...] = jnp.dot(middle, av_v[LANES : (bands - 1) * LANES, :], preferred_element_type=f32)

    def core_copies(c):
        return (
            remote(fbs.at[c, core], r1.at[c, 0], f_send.at[5 * c], f_recv.at[5 * c], to_core),
            remote(fbs.at[c, core_deep], r1.at[c, 1], f_send.at[5 * c + 1], f_recv.at[5 * c + 1], to_core),
        )

    def tile_copies(c):
        return (
            remote(s2.at[c, 0], r2.at[c, 0], f_send.at[5 * c + 2], f_recv.at[5 * c + 2], to_down),
            remote(s2.at[c, 1], r2.at[c, 1], f_send.at[5 * c + 3], f_recv.at[5 * c + 3], to_up),
        )

    def deep_copy(c):
        return remote(s3.at[c], r3.at[c], f_send.at[5 * c + 4], f_recv.at[5 * c + 4], to_deep)

    def stage_core(c):
        for copy in core_copies(c):
            copy.wait_recv()
        for k, group in enumerate((n, deep)):
            total = fbs[c, group].astype(f32) + r1[c, k].astype(f32)
            s2[c, 0, k] = total[0].astype(bf16)
            s2[c, 1, k] = total[2].astype(bf16)
            g1[c, k] = total[1]
        for copy in tile_copies(c):
            copy.start()

    def stage_tile(c):
        for copy in tile_copies(c):
            copy.wait_recv()
        s3[c] = (g1[c, 1] + r2[c, 0, 1].astype(f32) + r2[c, 1, 1].astype(f32)).astype(bf16)
        deep_copy(c).start()
        g1[c, 0] = g1[c, 0] + r2[c, 0, 0].astype(f32) + r2[c, 1, 0].astype(f32)

    def stage_deep(c):
        deep_copy(c).wait_recv()
        mine = cand[3 * n + 1, span(c), :].astype(f32)
        p_out[span(c), :] = (mine + (g1[c, 0] + r3[c].astype(f32))).astype(bf16)

    def channels_first(c):
        def body(i, carry):
            at = pl.ds(pl.multiple_of(c * part + i * 16, 16), 16)
            x_out[at] = jnp.swapaxes(xa[1 : rows + 1, at, :], 0, 1)
            return carry

        lax.fori_loop(0, part // 16, body, 0)

    with jax.named_scope("strip_wait"):
        pl.when(t > 0)(ring_up.wait_recv)
        pl.when(t < tiles - 1)(ring_down.wait_recv)

    def halo_strip(c):
        for side, row in ((0, 0), (1, rows + 1)):
            for q in range(per):
                begin, end = max(q * short, c * part), min((q + 1) * short, (c + 1) * part)
                if begin < end:
                    at = slice(begin, end)
                    fixed(row, at, placed(ring_v[side, begin - q * short : end - q * short, :], q))

    for c in range(parts):
        halo_sent(xa, 0, c)
    for c in range(parts):
        with jax.named_scope("second_halo_wait"):
            halo_arrived(xb, 1, c)
        with jax.named_scope("second_edges"):
            halo_strip(c)
            for r in (0, rows - 1):
                update_mid(r, c * part, part)
                update_out(r, c * part, part)
        at = slice(c * part, (c + 1) * part)
        with jax.named_scope("feedback_edges"):
            low_band = averaged(tops[0, at, :] + xa[1, at, :].astype(f32))
            high_band = averaged(tops[1, at, :] + xa[rows, at, :].astype(f32))
            terms = fb[at, :] + jnp.dot(low_band, av_v[:LANES, :], preferred_element_type=f32)
            terms = terms + jnp.dot(high_band, av_v[(bands - 1) * LANES :, :], preferred_element_type=f32)
        with jax.named_scope("feedback_slots"):
            for slot in range(3 * groups):
                total = jnp.zeros((part, LANES), f32)
                for k in range(slots):
                    total = total + (picks[0, 0, k] == slot).astype(f32) * terms[:, k * LANES : (k + 1) * LANES]
                fbs[c, slot // 3, slot % 3] = total.astype(bf16)
            for copy in core_copies(c):
                copy.start()
    for c in range(parts):
        with jax.named_scope("feedback_core"):
            stage_core(c)
        with jax.named_scope("channels_first"):
            channels_first(c)
    for c in range(parts):
        with jax.named_scope("feedback_tile"):
            stage_tile(c)
    for c in range(parts):
        with jax.named_scope("feedback_deep"):
            stage_deep(c)

    with jax.named_scope("sent"):
        tile_up.wait_send()
        tile_down.wait_send()
        for copy, _ in group_copies:
            copy.wait_send()

        @pl.when(inside)
        def _():
            for _, copy in group_copies:
                copy.wait_send()

        pl.when(ends)(over_up.wait_send)

        @pl.when(jnp.logical_or(after_first, before_last))
        def _():
            for copy in beside_up:
                copy.wait_send()
        onward.wait_send()
        pl.when(t < tiles - 1)(ring_up.wait_send)
        pl.when(t > 0)(ring_down.wait_send)
        for c in range(parts):
            halo_sent(xb, 1, c)
            for copy in core_copies(c):
                copy.wait_send()
            deep_copy(c).wait_send()
            for copy in tile_copies(c):
                copy.wait_send()


def write_out(pieces, x, p, nest_out, parent_out, sem):
    size = x.shape[0] // pieces
    copies = [pltpu.make_async_copy(p, parent_out, sem.at[pieces])]
    for c in range(pieces):
        at = pl.ds(c * size, size)
        copies.append(pltpu.make_async_copy(x.at[at], nest_out.at[0, at], sem.at[c]))
    for copy in copies:
        copy.start()
    for copy in copies:
        copy.wait()


def shards(nest_state, parent_state, mix_weight, intersection, interp_weight, avg_weight, land_mask):
    _, channels, rows, width = nest_state.shape
    groups, tiles = lax.axis_size("nest"), lax.axis_size("tile")
    slots = intersection.shape[2]
    cells = parent_state.shape[1]
    parts = 3
    part = channels // parts
    hbm = pl.BlockSpec(memory_space=pl.ANY)
    vmem = pl.BlockSpec(memory_space=pltpu.VMEM)
    x_new, p_new = pl.pallas_call(
        functools.partial(kernel, groups, tiles, parts),
        out_shape=(pltpu.VMEM((channels, rows, width), bf16), pltpu.VMEM((channels, cells), bf16)),
        in_specs=[pl.BlockSpec(memory_space=pltpu.SMEM)] + [hbm] * 6,
        out_specs=(vmem, vmem),
        scratch_shapes=[
            pltpu.VMEM((rows + 2, channels, width), bf16),
            pltpu.VMEM((rows + 2, channels, width), bf16),
            pltpu.VMEM((rows + 2, channels, 2 * LANES), bf16),
            pltpu.VMEM((rows, channels, 2 * LANES), bf16),
            pltpu.VMEM((3 * groups, channels, cells), bf16),
            pltpu.VMEM((channels, channels), bf16),
            pltpu.VMEM((slots, cells, width), bf16),
            pltpu.VMEM((width, slots * cells), bf16),
            pltpu.VMEM((rows, width), jnp.int32),
            pltpu.VMEM((2, rows, width), f32),
            pltpu.VMEM((channels, width), bf16),
            pltpu.VMEM((LANES // (2 * BW), LANES, 2 * LANES), bf16),
            pltpu.VMEM((2, channels * 2 * BW // LANES, LANES), bf16),
            pltpu.VMEM((2, channels * 2 * BW // LANES, LANES), bf16),
            pltpu.VMEM((width, LANES), bf16),
            pltpu.VMEM((2, channels, width), f32),
            pltpu.VMEM((channels, slots * cells), f32),
            pltpu.VMEM((parts, groups, 3, part, cells), bf16),
            pltpu.VMEM((parts, 2, 3, part, cells), bf16),
            pltpu.VMEM((parts, 2, 2, part, cells), bf16),
            pltpu.VMEM((parts, 2, 2, part, cells), bf16),
            pltpu.VMEM((parts, part, cells), bf16),
            pltpu.VMEM((parts, part, cells), bf16),
            pltpu.VMEM((parts, 2, part, cells), f32),
            pltpu.SemaphoreType.DMA((parts + 4 + slots,)),
            pltpu.SemaphoreType.DMA((12,)),
            pltpu.SemaphoreType.DMA((12,)),
            pltpu.SemaphoreType.DMA((4 * parts,)),
            pltpu.SemaphoreType.DMA((4 * parts,)),
            pltpu.SemaphoreType.DMA((2,)),
            pltpu.SemaphoreType.DMA((2,)),
            pltpu.SemaphoreType.DMA((5 * parts,)),
            pltpu.SemaphoreType.DMA((5 * parts,)),
        ],
        compiler_params=pltpu.CompilerParams(
            collective_id=0, has_side_effects=True, vmem_limit_bytes=48 * 2**20
        ),
    )(intersection, nest_state, parent_state, mix_weight, interp_weight, avg_weight, land_mask)
    return pl.pallas_call(
        functools.partial(write_out, 8),
        out_shape=(
            jax.ShapeDtypeStruct(nest_state.shape, bf16),
            jax.ShapeDtypeStruct(parent_state.shape, bf16),
        ),
        in_specs=[hbm, hbm],
        out_specs=(hbm, hbm),
        scratch_shapes=[pltpu.SemaphoreType.DMA((9,))],
        compiler_params=pltpu.CompilerParams(vmem_limit_bytes=8 * 2**20),
    )(x_new, p_new)


def solution(mesh):
    in_specs = (
        P("nest", None, "tile", None),
        P(None, ("nest", "tile")),
        P(),
        P("nest", "tile", None),
        P("nest", "tile", None, None, None),
        P("nest", "tile", None, None, None),
        P("nest", "tile", None),
    )
    out_specs = (P("nest", None, "tile", None), P(None, ("nest", "tile")))
    return jax.shard_map(shards, mesh=mesh, in_specs=in_specs, out_specs=out_specs, check_vma=False)
```

```python
import functools

import jax
import jax.numpy as jnp
from jax import lax
from jax.experimental import pallas as pl
from jax.experimental.pallas import tpu as pltpu
from jax.sharding import PartitionSpec as P

BW = 16
LANES = 128
SIDE = 4
MESH = pl.DeviceIdType.MESH
f32, bf16 = jnp.float32, jnp.bfloat16


def side_sum(x):
    zero = jnp.zeros((x.shape[0], 1), x.dtype)
    return jnp.concatenate([zero, x[:, :-1]], 1) + jnp.concatenate([x[:, 1:], zero], 1)


def kernel(
    groups, tiles, parts,
    picks, nest, parent, mix, interp, avg, land,
    x_out, p_out,
    xa, xb, xf, ws, cand, hub_v, m_v, w_v, av_v, land_v, coef, strip_v, place_v, pack_v, ring_v, pool_v, tops, fb, fbs, r1, s2, r2, s3, r3, g1,
    load_sem, p_send, p_recv, d_send, d_recv, h_send, h_recv, s_send, s_recv, f_send, f_recv,
):
    channels, rows, width = x_out.shape
    part = channels // parts
    slots = w_v.shape[0]
    bands = rows // 4
    n, t = lax.axis_index("nest"), lax.axis_index("tile")
    core = n + 1 - 2 * lax.rem(n, 2)
    deep = lax.rem(n + 2, groups)
    core_deep = lax.rem(core + 2, groups)
    up, down = lax.rem(t + 1, tiles), lax.rem(t + tiles - 1, tiles)
    to_up, to_down, to_core, to_deep = (n, up), (n, down), (core, t), (deep, t)
    first, last = t == 0, t == tiles - 1
    inside = jnp.logical_and(t > 0, t < tiles - 1)
    ends = jnp.logical_or(first, last)
    hub_tile = tiles // 2 + SIDE - 1
    hub = t == hub_tile

    def remote(src, dst, send, recv, device):
        return pltpu.make_async_remote_copy(
            src_ref=src, dst_ref=dst, send_sem=send, recv_sem=recv, device_id=device, device_id_type=MESH
        )

    barrier = pltpu.get_barrier_semaphore()

    def greet(device):
        pl.semaphore_signal(barrier, inc=1, device_id=device, device_id_type=MESH)

    greet(to_core)
    greet(to_deep)
    pl.when(t < tiles - 1)(lambda: greet(to_up))
    pl.when(t > 0)(lambda: greet(to_down))

    def span(c):
        return pl.ds(c * part, part)

    x_loads = [pltpu.make_async_copy(nest.at[0, span(c)], x_out.at[span(c)], load_sem.at[c]) for c in range(parts)]
    own_load = pltpu.make_async_copy(parent, cand.at[3 * n + 1], load_sem.at[parts])
    mix_load = pltpu.make_async_copy(mix, m_v, load_sem.at[parts + 1])
    land_load = pltpu.make_async_copy(land.at[0], land_v, load_sem.at[parts + 2])
    w_load = pltpu.make_async_copy(interp.at[0, 0], w_v, load_sem.at[parts + 3])
    av_loads = [
        pltpu.make_async_copy(avg.at[0, 0, k], av_v.at[:, k * LANES : (k + 1) * LANES], load_sem.at[parts + 4 + k])
        for k in range(slots)
    ]
    own_load.start()
    for load in x_loads:
        load.start()
    for load in (mix_load, land_load, w_load, *av_loads):
        load.start()
    def rows_first(c):
        x_loads[c].wait()

        def body(i, carry):
            at = pl.ds(pl.multiple_of(c * part + i * 16, 16), 16)
            xa[1 : rows + 1, at, :] = jnp.swapaxes(x_out[at], 0, 1)
            return carry

        lax.fori_loop(0, part // 16, body, 0)

    @pl.when(first)
    def _():
        pl.semaphore_wait(barrier, 3)
        greet(to_down)
        greet((deep, down))

    @pl.when(inside)
    def _():
        pl.semaphore_wait(barrier, 4)

    @pl.when(hub)
    def _():
        greet((n, tiles - 1))
        greet((deep, tiles - 1))

    @pl.when(last)
    def _():
        pl.semaphore_wait(barrier, 7)
        greet(to_up)
        greet((deep, up))
        greet((n, hub_tile))
        greet((deep, hub_tile))

    own_load.wait()
    own = cand.at[3 * n + 1]
    tile_up = remote(own, cand.at[3 * n], p_send.at[0], p_recv.at[0], to_up)
    tile_down = remote(own, cand.at[3 * n + 2], p_send.at[1], p_recv.at[1], to_down)

    def to_groups(o):
        mine = cand.at[3 * n + o]
        return (
            remote(mine, mine, p_send.at[2 + o], p_recv.at[2 + o], to_core),
            remote(mine, mine, p_send.at[5 + o], p_recv.at[5 + o], to_deep),
        )

    group_copies = [to_groups(o) for o in range(3)]

    over_up = remote(own, cand.at[3 * n], p_send.at[9], p_recv.at[9], (deep, up))
    over_down = remote(own, cand.at[3 * n + 2], p_send.at[9], p_recv.at[9], (deep, down))
    def beside(k, source, target, device):
        return remote(cand.at[3 * deep + source], cand.at[3 * deep + target], p_send.at[10 + k], p_recv.at[10 + k], device)

    beside_down = beside(0, 1, 2, to_down), beside(1, 0, 1, to_down)
    after_first = t == 1
    to_hub = [
        remote(cand.at[3 * n + 1 - k], hub_v.at[k], d_send.at[k], d_recv.at[k], (deep, hub_tile)) for k in range(2)
    ]
    from_hub = [
        remote(hub_v.at[k], cand.at[3 * deep + 1 - k], d_send.at[2 + k], d_recv.at[2 + k], (n, tiles - 1))
        for k in range(2)
    ]

    def hub_pass(k):
        to_hub[k].wait_recv()
        from_hub[k].start()

    def pass_on(o):
        group_copies[o][0].start()
        pl.when(inside)(group_copies[o][1].start)

    def from_below():
        tile_up.wait_recv()
        pass_on(0)

    def from_above():
        tile_down.wait_recv()
        pass_on(2)

    with jax.named_scope("own_tile"):
        pl.when(last)(to_hub[0].start)
        tile_up.start()
        pl.when(t > 0)(tile_down.start)
        pass_on(1)

    def halo_up(state, step, c):
        k = (step * parts + c) * 2
        return remote(state.at[rows, span(c)], state.at[0, span(c)], h_send.at[k], h_recv.at[k], to_up)

    def halo_down(state, step, c):
        k = (step * parts + c) * 2 + 1
        return remote(state.at[1, span(c)], state.at[rows + 1, span(c)], h_send.at[k], h_recv.at[k], to_down)

    def halos(state, step, c):
        return halo_up(state, step, c), halo_down(state, step, c)

    def halo_start(state, step, c):
        upward, downward = halos(state, step, c)
        pl.when(t < tiles - 1)(upward.start)
        pl.when(t > 0)(downward.start)

    def halo_one_way(state, step, c):
        upward, downward = halos(state, step, c)
        pl.when(t < tiles - 1)(upward.start)
        pl.when(t > 1)(downward.start)

    def halo_held(state, step, c):
        pl.when(after_first)(halo_down(state, step, c).start)

    def halo_arrived(state, step, c):
        upward, downward = halos(state, step, c)
        pl.when(t > 0)(upward.wait_recv)
        pl.when(t < tiles - 1)(downward.wait_recv)

    def halo_sent(state, step, c):
        upward, downward = halos(state, step, c)
        pl.when(t < tiles - 1)(upward.wait_send)
        pl.when(t > 0)(downward.wait_send)

    @pl.when(first)
    def _():
        ring_v[0] = jnp.zeros(ring_v.shape[1:], bf16)
        for state in (xa, xb):
            state[0] = jnp.zeros((channels, width), bf16)

    @pl.when(last)
    def _():
        ring_v[1] = jnp.zeros(ring_v.shape[1:], bf16)
        for state in (xa, xb):
            state[rows + 1] = jnp.zeros((channels, width), bf16)

    with jax.named_scope("rows_first"):
        for c in range(parts):
            rows_first(c)
            (halo_start if c < parts - 1 else halo_one_way)(xa, 0, c)

    source = lax.broadcasted_iota(jnp.int32, (LANES, 2 * LANES), 0)
    target = lax.broadcasted_iota(jnp.int32, (LANES, 2 * LANES), 1)
    west_at = jnp.where(target < BW, target, -LANES)
    east_at = jnp.where(target >= 2 * LANES - BW, target - (2 * LANES - 2 * BW), -LANES)
    weight = jnp.where(target < BW, BW - target, target - (2 * LANES - BW - 1)).astype(f32) / BW
    for j in range(LANES // (2 * BW)):
        here = source - j * 2 * BW
        place_v[j] = jnp.where((here == west_at) | (here == east_at), weight, 0.0).astype(bf16)

    land_load.wait()
    mix_load.wait()
    column = lax.broadcasted_iota(jnp.int32, (rows, width), 1)
    edge = jnp.minimum(column, width - 1 - column)
    ramp = jnp.maximum(BW - edge, 0).astype(f32) / BW
    factor = jnp.where(land_v[...] == 1, 0.5, 1.0)
    coef[0] = (1.0 - ramp) * (1.0 - 0.9 * factor)
    coef[1] = (1.0 - ramp) * (0.4 * factor)

    def new_value(x, above, below, sides, mixed, mine, around):
        near = above + below + jnp.asarray(0.125, bf16) * sides
        return mine * x.astype(f32) + around * (near.astype(f32) + 1.25 * mixed)

    def update(r, start, count):
        mixed = jnp.dot(m_v[start : start + count, :], xa[r + 1], preferred_element_type=f32)
        mine, around = coef[0, pl.ds(r, 1), :], coef[1, pl.ds(r, 1), :]
        for s in range(0, count, 16):
            at = slice(start + s, start + s + 16)
            x = xa[r + 1, at, :]
            y = new_value(x, xa[r, at, :], xa[r + 2, at, :], side_sum(x), mixed[s : s + 16], mine, around)
            xb[r + 1, at, :] = y.astype(bf16)

    def first_rows(begin, end):
        def body(i, carry):
            update(2 * i + 1, 0, channels)
            update(2 * i + 2, 0, channels)
            return carry

        lax.fori_loop(begin, end, body, 0)

    row_start, row_end = lax.rem(t, SIDE) == 0, lax.rem(t, SIDE) == SIDE - 1
    beside_row = jnp.logical_or(row_start, row_end)
    far = jnp.logical_or(t == tiles // 2 - 1, t == tiles // 2)
    strip_early = jnp.logical_or(ends, far)
    with jax.named_scope("first_inner"):
        first_rows(0, 3)
    with jax.named_scope("tile_on"):
        pl.when(after_first)(from_below)
        pl.when(jnp.logical_not(row_end))(from_above)
        pl.when(jnp.logical_not(jnp.logical_or(row_start, after_first)))(from_below)


        @pl.when(last)
        def _():
            to_hub[1].start()
            over_up.start()

        @pl.when(after_first)
        def _():
            group_copies[1][1].wait_recv()
            beside_down[0].start()

    with jax.named_scope("first_inner"):
        first_rows(3, (rows - 2) // 2)

    mid, low, high = slice(LANES, width - LANES), slice(0, LANES), slice(width - LANES, width)

    def update_mid(r, start, count):
        mixed = jnp.dot(m_v[start : start + count, :], xb[r + 1, :, mid], preferred_element_type=f32)
        mine, around = coef[0, pl.ds(r, 1), :][:, mid], coef[1, pl.ds(r, 1), :][:, mid]
        for s in range(0, count, 16):
            at = slice(start + s, start + s + 16)
            x = xb[r + 1, at, :]
            sides = side_sum(x)[:, mid]
            y = new_value(x[:, mid], xb[r, at, mid], xb[r + 2, at, mid], sides, mixed[s : s + 16], mine, around)
            xa[r + 1, at, mid] = y.astype(bf16)

    def update_out(r, start, count):
        mixed = jnp.dot(m_v[start : start + count, :], xf[r + 1], preferred_element_type=f32)
        mine, around = [
            jnp.concatenate([row[:, low], row[:, high]], axis=1) for row in (coef[0, pl.ds(r, 1), :], coef[1, pl.ds(r, 1), :])
        ]
        for s in range(0, count, 16):
            at = slice(start + s, start + s + 16)
            x = xf[r + 1, at, :]
            whole = side_sum(jnp.concatenate([x[:, :LANES], xb[r + 1, at, mid], x[:, LANES:]], axis=1))
            sides = jnp.concatenate([whole[:, low], whole[:, high]], axis=1)
            y = new_value(x, xf[r, at, :], xf[r + 2, at, :], sides, mixed[s : s + 16], mine, around)
            y = (y + ws[r, at, :].astype(f32)).astype(bf16)
            xa[r + 1, at, low] = y[:, :LANES]
            xa[r + 1, at, high] = y[:, LANES:]

    def quads(one_row, row, begin, end, start, count):
        def body(i, carry):
            for j in range(4):
                one_row(row + 4 * i + j, start, count)
            return carry

        lax.fori_loop(begin, end, body, 0)

    onward = [
        remote(cand.at[3 * deep + o], cand.at[3 * deep + o], d_send.at[4 + o], d_recv.at[4 + o], to_core) for o in range(3)
    ]

    def deep_tiles():
        @pl.when(jnp.logical_not(after_first))
        def _():
            group_copies[1][1].wait_recv()
            group_copies[0][1].wait_recv()

        onward[1].start()
        onward[0].start()
        group_copies[2][1].wait_recv()
        onward[2].start()

    def middle_quads(begin, end):
        with jax.named_scope("second_middle"):
            quads(update_mid, 2, begin, end, 0, channels)

    early = jnp.where(beside_row, 1, 0)
    sooner = jnp.where(far, 3, early)
    later = jnp.where(far, 3, early + 1)

    def first_edges(c):
        with jax.named_scope("first_halo_wait"):
            halo_arrived(xa, 0, c)
        with jax.named_scope("first_edges"):
            update(0, c * part, part)
            update(rows - 1, c * part, part)

    middle_quads(0, early)
    with jax.named_scope("tile_on"):
        pl.when(jnp.logical_and(row_end, t < tiles - 1))(from_above)
        pl.when(jnp.logical_and(row_start, t > 0))(from_below)

        @pl.when(hub)
        def _():
            pl.semaphore_wait(barrier, 2)
            hub_pass(0)

        @pl.when(first)
        def _():
            pl.semaphore_wait(barrier, 2)
            tile_down.start()
            over_down.start()

    middle_quads(early, sooner)
    first_edges(0)
    with jax.named_scope("tile_on"):

        @pl.when(after_first)
        def _():
            group_copies[0][1].wait_recv()
            beside_down[1].start()

        halo_held(xa, 0, parts - 1)

    halo_start(xb, 1, 0)
    middle_quads(sooner, later)
    with jax.named_scope("deep_tiles_wait"):
        pl.when(hub)(lambda: hub_pass(1))
        pl.when(jnp.logical_and(inside, beside_row))(deep_tiles)
    first_edges(1)
    middle_quads(later, 2)
    with jax.named_scope("deep_tiles_wait"):
        pl.when(jnp.logical_not(beside_row))(deep_tiles)
    middle_quads(jnp.maximum(later, 2), 3)
    with jax.named_scope("tile_on"):
        pl.when(first)(from_below)
        pl.when(last)(from_above)

    cells = 2 * BW
    per = LANES // cells
    short = channels // per

    def pack(begin):
        return jnp.concatenate([strip_v[q * short : (q + 1) * short, begin : begin + cells] for q in range(per)], axis=1)

    ring_up = remote(pack_v.at[0], ring_v.at[0], s_send.at[0], s_recv.at[0], to_up)
    ring_down = remote(pack_v.at[1], ring_v.at[1], s_send.at[1], s_recv.at[1], to_down)

    def boundary_strip():
        with jax.named_scope("deep_tiles_wait"):

            @pl.when(first)
            def _():
                beside_down[0].wait_recv()
                onward[2].start()
                beside_down[1].wait_recv()
                onward[1].start()
                over_up.wait_recv()
                onward[0].start()

            @pl.when(last)
            def _():
                from_hub[0].wait_recv()
                onward[1].start()
                from_hub[1].wait_recv()
                onward[0].start()
                over_down.wait_recv()
                onward[2].start()

        with jax.named_scope("core_tiles_wait"):
            for o in range(3):
                group_copies[o][0].wait_recv()
            for copy in onward:
                copy.wait_recv()
        with jax.named_scope("strip"):
            picked = jnp.concatenate([cand[picks[0, 0, k]] for k in range(slots)], axis=1)
            weights = w_v[...].reshape(slots * LANES, width)
            strip_v[...] = jnp.dot(picked, weights, preferred_element_type=f32).astype(bf16)
        with jax.named_scope("strip_send"):
            pack_v[0] = pack(width - cells)
            pack_v[1] = pack(0)
            pl.when(t < tiles - 1)(ring_up.start)
            pl.when(t > 0)(ring_down.start)
            halo_start(xb, 1, 1)

    def placed(value, j):
        return jnp.dot(value, place_v[j], preferred_element_type=f32)

    def fixed(row, at, wide):
        xf[row, at, :LANES] = (xb[row, at, low].astype(f32) + wide[:, :LANES]).astype(bf16)
        xf[row, at, LANES:] = (xb[row, at, high].astype(f32) + wide[:, LANES:]).astype(bf16)

    everything = slice(0, channels)

    def spread_strip():
        def spread(j, carry):
            value = jnp.concatenate([strip_v[:, b * LANES : (b + 1) * LANES] for b in range(rows // per)], axis=0)
            wide = placed(value, j)
            for b in range(rows // per):
                block = wide[b * channels : (b + 1) * channels]
                ws[per * b + j] = block.astype(bf16)
                fixed(per * b + j + 1, everything, block)
            return carry

        with jax.named_scope("strip_spread"):
            lax.fori_loop(0, per, spread, 0)

    most = channels - part

    def outer_quads(start, count):
        with jax.named_scope("second_outer"):
            quads(update_out, 2, 0, (rows - 4) // 4, start, count)

    def outer_near(start, count):
        with jax.named_scope("second_outer"):
            update_out(1, start, count)
            update_out(rows - 2, start, count)

    w_load.wait()

    pl.when(strip_early)(boundary_strip)

    @pl.when(ends)
    def _():
        spread_strip()
        outer_quads(0, most)

    first_edges(parts - 1)
    with jax.named_scope("second_middle"):
        update_mid(1, 0, channels)
        update_mid(rows - 2, 0, channels)
    pl.when(jnp.logical_not(strip_early))(boundary_strip)
    halo_start(xb, 1, parts - 1)

    @pl.when(ends)
    def _():
        with jax.named_scope("strip_spread"):
            for r in (0, rows - 1):
                fixed(r + 1, everything, ws[r].astype(f32))

    @pl.when(inside)
    def _():
        spread_strip()
        outer_quads(0, most)

    outer_near(0, most)

    for load in av_loads:
        load.wait()
    pool_row = lax.broadcasted_iota(jnp.int32, (width, LANES), 0)
    pool_col = lax.broadcasted_iota(jnp.int32, (width, LANES), 1)
    pool_v[...] = jnp.where(pool_row // 4 == pool_col, 1.0 / 16.0, 0.0).astype(bf16)

    def row_total(begin, count, at):
        total = xa[begin + 1, at, :].astype(f32)
        for j in range(1, count):
            total = total + xa[begin + 1 + j, at, :].astype(f32)
        return total

    def averaged(total):
        return jnp.dot(total.astype(bf16), pool_v[...], preferred_element_type=f32).astype(bf16)

    def feedback_inner(start, count):
        with jax.named_scope("feedback_inner"):
            at = slice(start, start + count)
            tops[0, at] = row_total(1, 3, at)
            tops[1, at] = row_total(rows - 4, 3, at)
            middle = jnp.concatenate([averaged(row_total(4 * b, 4, at)) for b in range(1, bands - 1)], axis=1)
            fb[at] = jnp.dot(middle, av_v[LANES : (bands - 1) * LANES, :], preferred_element_type=f32)

    def core_copies(c):
        return (
            remote(fbs.at[c, core], r1.at[c, 0], f_send.at[5 * c], f_recv.at[5 * c], to_core),
            remote(fbs.at[c, core_deep], r1.at[c, 1], f_send.at[5 * c + 1], f_recv.at[5 * c + 1], to_core),
        )

    def tile_copies(c):
        return (
            remote(s2.at[c, 0], r2.at[c, 0], f_send.at[5 * c + 2], f_recv.at[5 * c + 2], to_down),
            remote(s2.at[c, 1], r2.at[c, 1], f_send.at[5 * c + 3], f_recv.at[5 * c + 3], to_up),
        )

    def deep_copy(c):
        return remote(s3.at[c], r3.at[c], f_send.at[5 * c + 4], f_recv.at[5 * c + 4], to_deep)

    def stage_core(c):
        for copy in core_copies(c):
            copy.wait_recv()
        for k, group in enumerate((n, deep)):
            total = fbs[c, group].astype(f32) + r1[c, k].astype(f32)
            s2[c, 0, k] = total[0].astype(bf16)
            s2[c, 1, k] = total[2].astype(bf16)
            g1[c, k] = total[1]
        for copy in tile_copies(c):
            copy.start()

    def stage_tile(c):
        for copy in tile_copies(c):
            copy.wait_recv()
        s3[c] = (g1[c, 1] + r2[c, 0, 1].astype(f32) + r2[c, 1, 1].astype(f32)).astype(bf16)
        deep_copy(c).start()
        g1[c, 0] = g1[c, 0] + r2[c, 0, 0].astype(f32) + r2[c, 1, 0].astype(f32)

    def stage_deep(c):
        deep_copy(c).wait_recv()
        mine = cand[3 * n + 1, span(c), :].astype(f32)
        p_out[span(c), :] = (mine + (g1[c, 0] + r3[c].astype(f32))).astype(bf16)

    def channels_first(c):
        def body(i, carry):
            at = pl.ds(pl.multiple_of(c * part + i * 16, 16), 16)
            x_out[at] = jnp.swapaxes(xa[1 : rows + 1, at, :], 0, 1)
            return carry

        lax.fori_loop(0, part // 16, body, 0)

    feedback_inner(0, most)

    with jax.named_scope("strip_wait"):
        pl.when(t > 0)(ring_up.wait_recv)
        pl.when(t < tiles - 1)(ring_down.wait_recv)

    def halo_strip(c):
        for side, row in ((0, 0), (1, rows + 1)):
            for q in range(per):
                begin, end = max(q * short, c * part), min((q + 1) * short, (c + 1) * part)
                if begin < end:
                    at = slice(begin, end)
                    fixed(row, at, placed(ring_v[side, begin - q * short : end - q * short, :], q))

    for c in range(parts):
        halo_sent(xa, 0, c)
    for c in range(parts):
        if c == parts - 1:
            outer_quads(c * part, part)
            outer_near(c * part, part)
            feedback_inner(c * part, part)
            with jax.named_scope("feedback_core"):
                for k in range(c):
                    stage_core(k)
        with jax.named_scope("second_halo_wait"):
            halo_arrived(xb, 1, c)
        with jax.named_scope("second_edges"):
            halo_strip(c)
            for r in (0, rows - 1):
                update_mid(r, c * part, part)
                update_out(r, c * part, part)
        at = slice(c * part, (c + 1) * part)
        with jax.named_scope("feedback_edges"):
            low_band = averaged(tops[0, at, :] + xa[1, at, :].astype(f32))
            high_band = averaged(tops[1, at, :] + xa[rows, at, :].astype(f32))
            terms = fb[at, :] + jnp.dot(low_band, av_v[:LANES, :], preferred_element_type=f32)
            terms = terms + jnp.dot(high_band, av_v[(bands - 1) * LANES :, :], preferred_element_type=f32)
        with jax.named_scope("feedback_slots"):
            for slot in range(3 * groups):
                total = jnp.zeros((part, LANES), f32)
                for k in range(slots):
                    total = total + (picks[0, 0, k] == slot).astype(f32) * terms[:, k * LANES : (k + 1) * LANES]
                fbs[c, slot // 3, slot % 3] = total.astype(bf16)
            for copy in core_copies(c):
                copy.start()
    with jax.named_scope("channels_first"):
        channels_first(0)
    with jax.named_scope("feedback_core"):
        stage_core(parts - 1)
    with jax.named_scope("channels_first"):
        for c in range(1, parts):
            channels_first(c)
    for c in range(parts):
        with jax.named_scope("feedback_tile"):
            stage_tile(c)
    for c in range(parts):
        with jax.named_scope("feedback_deep"):
            stage_deep(c)

    with jax.named_scope("sent"):
        tile_up.wait_send()
        tile_down.wait_send()
        for copy, _ in group_copies:
            copy.wait_send()

        @pl.when(inside)
        def _():
            for _, copy in group_copies:
                copy.wait_send()

        pl.when(ends)(over_up.wait_send)

        @pl.when(after_first)
        def _():
            for copy in beside_down:
                copy.wait_send()

        @pl.when(last)
        def _():
            for copy in to_hub:
                copy.wait_send()

        @pl.when(hub)
        def _():
            for copy in from_hub:
                copy.wait_send()
        for copy in onward:
            copy.wait_send()
        pl.when(t < tiles - 1)(ring_up.wait_send)
        pl.when(t > 0)(ring_down.wait_send)
        for c in range(parts):
            halo_sent(xb, 1, c)
            for copy in core_copies(c):
                copy.wait_send()
            deep_copy(c).wait_send()
            for copy in tile_copies(c):
                copy.wait_send()


def write_out(pieces, x, p, nest_out, parent_out, sem):
    size = x.shape[0] // pieces
    copies = [pltpu.make_async_copy(p, parent_out, sem.at[pieces])]
    for c in range(pieces):
        at = pl.ds(c * size, size)
        copies.append(pltpu.make_async_copy(x.at[at], nest_out.at[0, at], sem.at[c]))
    for copy in copies:
        copy.start()
    for copy in copies:
        copy.wait()


def shards(nest_state, parent_state, mix_weight, intersection, interp_weight, avg_weight, land_mask):
    _, channels, rows, width = nest_state.shape
    groups, tiles = lax.axis_size("nest"), lax.axis_size("tile")
    slots = intersection.shape[2]
    cells = parent_state.shape[1]
    parts = 3
    part = channels // parts
    hbm = pl.BlockSpec(memory_space=pl.ANY)
    vmem = pl.BlockSpec(memory_space=pltpu.VMEM)
    x_new, p_new = pl.pallas_call(
        functools.partial(kernel, groups, tiles, parts),
        out_shape=(pltpu.VMEM((channels, rows, width), bf16), pltpu.VMEM((channels, cells), bf16)),
        in_specs=[pl.BlockSpec(memory_space=pltpu.SMEM)] + [hbm] * 6,
        out_specs=(vmem, vmem),
        scratch_shapes=[
            pltpu.VMEM((rows + 2, channels, width), bf16),
            pltpu.VMEM((rows + 2, channels, width), bf16),
            pltpu.VMEM((rows + 2, channels, 2 * LANES), bf16),
            pltpu.VMEM((rows, channels, 2 * LANES), bf16),
            pltpu.VMEM((3 * groups, channels, cells), bf16),
            pltpu.VMEM((2, channels, cells), bf16),
            pltpu.VMEM((channels, channels), bf16),
            pltpu.VMEM((slots, cells, width), bf16),
            pltpu.VMEM((width, slots * cells), bf16),
            pltpu.VMEM((rows, width), jnp.int32),
            pltpu.VMEM((2, rows, width), f32),
            pltpu.VMEM((channels, width), bf16),
            pltpu.VMEM((LANES // (2 * BW), LANES, 2 * LANES), bf16),
            pltpu.VMEM((2, channels * 2 * BW // LANES, LANES), bf16),
            pltpu.VMEM((2, channels * 2 * BW // LANES, LANES), bf16),
            pltpu.VMEM((width, LANES), bf16),
            pltpu.VMEM((2, channels, width), f32),
            pltpu.VMEM((channels, slots * cells), f32),
            pltpu.VMEM((parts, groups, 3, part, cells), bf16),
            pltpu.VMEM((parts, 2, 3, part, cells), bf16),
            pltpu.VMEM((parts, 2, 2, part, cells), bf16),
            pltpu.VMEM((parts, 2, 2, part, cells), bf16),
            pltpu.VMEM((parts, part, cells), bf16),
            pltpu.VMEM((parts, part, cells), bf16),
            pltpu.VMEM((parts, 2, part, cells), f32),
            pltpu.SemaphoreType.DMA((parts + 4 + slots,)),
            pltpu.SemaphoreType.DMA((12,)),
            pltpu.SemaphoreType.DMA((12,)),
            pltpu.SemaphoreType.DMA((7,)),
            pltpu.SemaphoreType.DMA((7,)),
            pltpu.SemaphoreType.DMA((4 * parts,)),
            pltpu.SemaphoreType.DMA((4 * parts,)),
            pltpu.SemaphoreType.DMA((2,)),
            pltpu.SemaphoreType.DMA((2,)),
            pltpu.SemaphoreType.DMA((5 * parts,)),
            pltpu.SemaphoreType.DMA((5 * parts,)),
        ],
        compiler_params=pltpu.CompilerParams(
            collective_id=0, has_side_effects=True, vmem_limit_bytes=48 * 2**20
        ),
    )(intersection, nest_state, parent_state, mix_weight, interp_weight, avg_weight, land_mask)
    return pl.pallas_call(
        functools.partial(write_out, 8),
        out_shape=(
            jax.ShapeDtypeStruct(nest_state.shape, bf16),
            jax.ShapeDtypeStruct(parent_state.shape, bf16),
        ),
        in_specs=[hbm, hbm],
        out_specs=(hbm, hbm),
        scratch_shapes=[pltpu.SemaphoreType.DMA((9,))],
        compiler_params=pltpu.CompilerParams(vmem_limit_bytes=8 * 2**20),
    )(x_new, p_new)


def solution(mesh):
    in_specs = (
        P("nest", None, "tile", None),
        P(None, ("nest", "tile")),
        P(),
        P("nest", "tile", None),
        P("nest", "tile", None, None, None),
        P("nest", "tile", None, None, None),
        P("nest", "tile", None),
    )
    out_specs = (P("nest", None, "tile", None), P(None, ("nest", "tile")))
    return jax.shard_map(shards, mesh=mesh, in_specs=in_specs, out_specs=out_specs, check_vma=False)
```

```python
import functools

import jax
import jax.numpy as jnp
from jax import lax
from jax.experimental import pallas as pl
from jax.experimental.pallas import tpu as pltpu
from jax.sharding import PartitionSpec as P

BW = 16
LANES = 128
SIDE = 4
MESH = pl.DeviceIdType.MESH
f32, bf16 = jnp.float32, jnp.bfloat16


def side_sum(x):
    zero = jnp.zeros((x.shape[0], 1), x.dtype)
    return jnp.concatenate([zero, x[:, :-1]], 1) + jnp.concatenate([x[:, 1:], zero], 1)


def kernel(
    groups, tiles, parts,
    picks, nest, parent, mix, interp, avg, land,
    x_out, p_out,
    xa, xb, xf, ws, cand, hub_v, m_v, w_v, av_v, land_v, coef, strip_v, place_v, pack_v, ring_v, pool_v, tops, fb, fbs, r1, s2, r2, s3, r3, g1,
    load_sem, p_send, p_recv, d_send, d_recv, h_send, h_recv, s_send, s_recv, f_send, f_recv,
):
    channels, rows, width = x_out.shape
    part = channels // parts
    slots = w_v.shape[0]
    bands = rows // 4
    n, t = lax.axis_index("nest"), lax.axis_index("tile")
    core = n + 1 - 2 * lax.rem(n, 2)
    deep = lax.rem(n + 2, groups)
    core_deep = lax.rem(core + 2, groups)
    up, down = lax.rem(t + 1, tiles), lax.rem(t + tiles - 1, tiles)
    to_up, to_down, to_core, to_deep = (n, up), (n, down), (core, t), (deep, t)
    first, last = t == 0, t == tiles - 1
    inside = jnp.logical_and(t > 0, t < tiles - 1)
    ends = jnp.logical_or(first, last)
    over_above = jnp.logical_or(t == tiles // 2 - 1, last)
    over_below = jnp.logical_or(t == tiles // 2, first)
    far = jnp.logical_or(t == tiles // 2 - 1, t == tiles // 2)
    hub_tile = tiles // 2 + SIDE - 1
    hub = t == hub_tile

    def remote(src, dst, send, recv, device):
        return pltpu.make_async_remote_copy(
            src_ref=src, dst_ref=dst, send_sem=send, recv_sem=recv, device_id=device, device_id_type=MESH
        )

    barrier = pltpu.get_barrier_semaphore()

    def greet(device):
        pl.semaphore_signal(barrier, inc=1, device_id=device, device_id_type=MESH)

    greet(to_core)
    greet(to_deep)
    pl.when(t < tiles - 1)(lambda: greet(to_up))
    pl.when(t > 0)(lambda: greet(to_down))
    pl.when(t == tiles // 2 - 1)(lambda: greet((deep, up)))
    pl.when(t == tiles // 2)(lambda: greet((deep, down)))

    def span(c):
        return pl.ds(c * part, part)

    x_loads = [pltpu.make_async_copy(nest.at[0, span(c)], x_out.at[span(c)], load_sem.at[c]) for c in range(parts)]
    own_load = pltpu.make_async_copy(parent, cand.at[3 * n + 1], load_sem.at[parts])
    mix_load = pltpu.make_async_copy(mix, m_v, load_sem.at[parts + 1])
    land_load = pltpu.make_async_copy(land.at[0], land_v, load_sem.at[parts + 2])
    w_load = pltpu.make_async_copy(interp.at[0, 0], w_v, load_sem.at[parts + 3])
    av_loads = [
        pltpu.make_async_copy(avg.at[0, 0, k], av_v.at[:, k * LANES : (k + 1) * LANES], load_sem.at[parts + 4 + k])
        for k in range(slots)
    ]
    own_load.start()
    for load in x_loads:
        load.start()
    for load in (mix_load, land_load, w_load, *av_loads):
        load.start()
    def rows_first(c):
        x_loads[c].wait()

        def body(i, carry):
            at = pl.ds(pl.multiple_of(c * part + i * 16, 16), 16)
            xa[1 : rows + 1, at, :] = jnp.swapaxes(x_out[at], 0, 1)
            return carry

        lax.fori_loop(0, part // 16, body, 0)

    @pl.when(first)
    def _():
        pl.semaphore_wait(barrier, 3)
        greet(to_down)
        greet((deep, down))

    @pl.when(jnp.logical_and(inside, jnp.logical_not(far)))
    def _():
        pl.semaphore_wait(barrier, 4)

    @pl.when(far)
    def _():
        pl.semaphore_wait(barrier, 5)

    @pl.when(hub)
    def _():
        greet((n, tiles - 1))
        greet((deep, tiles - 1))

    @pl.when(last)
    def _():
        pl.semaphore_wait(barrier, 7)
        greet(to_up)
        greet((deep, up))
        greet((n, hub_tile))
        greet((deep, hub_tile))

    own_load.wait()
    own = cand.at[3 * n + 1]
    tile_up = remote(own, cand.at[3 * n], p_send.at[0], p_recv.at[0], to_up)
    tile_down = remote(own, cand.at[3 * n + 2], p_send.at[1], p_recv.at[1], to_down)

    def to_groups(o):
        mine = cand.at[3 * n + o]
        return (
            remote(mine, mine, p_send.at[2 + o], p_recv.at[2 + o], to_core),
            remote(mine, mine, p_send.at[5 + o], p_recv.at[5 + o], to_deep),
        )

    group_copies = [to_groups(o) for o in range(3)]

    over_up = remote(own, cand.at[3 * n], p_send.at[9], p_recv.at[9], (deep, up))
    over_down = remote(own, cand.at[3 * n + 2], p_send.at[9], p_recv.at[9], (deep, down))
    def beside(k, source, target, device):
        return remote(cand.at[3 * deep + source], cand.at[3 * deep + target], p_send.at[10 + k], p_recv.at[10 + k], device)

    beside_down = beside(0, 1, 2, to_down), beside(1, 0, 1, to_down)
    after_first = t == 1
    to_hub = [
        remote(cand.at[3 * n + 1 - k], hub_v.at[k], d_send.at[k], d_recv.at[k], (deep, hub_tile)) for k in range(2)
    ]
    from_hub = [
        remote(hub_v.at[k], cand.at[3 * deep + 1 - k], d_send.at[2 + k], d_recv.at[2 + k], (n, tiles - 1))
        for k in range(2)
    ]

    def hub_pass(k):
        to_hub[k].wait_recv()
        from_hub[k].start()

    def pass_on(o):
        group_copies[o][0].start()
        pl.when(inside)(group_copies[o][1].start)

    def from_below():
        tile_up.wait_recv()
        pass_on(0)

    def from_above():
        tile_down.wait_recv()
        pass_on(2)

    with jax.named_scope("own_tile"):
        pl.when(last)(to_hub[0].start)
        tile_up.start()
        pl.when(t > 0)(tile_down.start)
        pass_on(1)

    def halo_up(state, step, c):
        k = (step * parts + c) * 2
        return remote(state.at[rows, span(c)], state.at[0, span(c)], h_send.at[k], h_recv.at[k], to_up)

    def halo_down(state, step, c):
        k = (step * parts + c) * 2 + 1
        return remote(state.at[1, span(c)], state.at[rows + 1, span(c)], h_send.at[k], h_recv.at[k], to_down)

    def halos(state, step, c):
        return halo_up(state, step, c), halo_down(state, step, c)

    def halo_start(state, step, c):
        upward, downward = halos(state, step, c)
        pl.when(t < tiles - 1)(upward.start)
        pl.when(t > 0)(downward.start)

    def halo_one_way(state, step, c):
        upward, downward = halos(state, step, c)
        pl.when(t < tiles - 1)(upward.start)
        pl.when(t > 1)(downward.start)

    def halo_held(state, step, c):
        pl.when(after_first)(halo_down(state, step, c).start)

    def halo_arrived(state, step, c):
        upward, downward = halos(state, step, c)
        pl.when(t > 0)(upward.wait_recv)
        pl.when(t < tiles - 1)(downward.wait_recv)

    def halo_sent(state, step, c):
        upward, downward = halos(state, step, c)
        pl.when(t < tiles - 1)(upward.wait_send)
        pl.when(t > 0)(downward.wait_send)

    @pl.when(first)
    def _():
        ring_v[0] = jnp.zeros(ring_v.shape[1:], bf16)
        for state in (xa, xb):
            state[0] = jnp.zeros((channels, width), bf16)

    @pl.when(last)
    def _():
        ring_v[1] = jnp.zeros(ring_v.shape[1:], bf16)
        for state in (xa, xb):
            state[rows + 1] = jnp.zeros((channels, width), bf16)

    with jax.named_scope("rows_first"):
        for c in range(parts):
            rows_first(c)
            (halo_start if c < parts - 1 else halo_one_way)(xa, 0, c)

    source = lax.broadcasted_iota(jnp.int32, (LANES, 2 * LANES), 0)
    target = lax.broadcasted_iota(jnp.int32, (LANES, 2 * LANES), 1)
    west_at = jnp.where(target < BW, target, -LANES)
    east_at = jnp.where(target >= 2 * LANES - BW, target - (2 * LANES - 2 * BW), -LANES)
    weight = jnp.where(target < BW, BW - target, target - (2 * LANES - BW - 1)).astype(f32) / BW
    for j in range(LANES // (2 * BW)):
        here = source - j * 2 * BW
        place_v[j] = jnp.where((here == west_at) | (here == east_at), weight, 0.0).astype(bf16)

    land_load.wait()
    mix_load.wait()
    column = lax.broadcasted_iota(jnp.int32, (rows, width), 1)
    edge = jnp.minimum(column, width - 1 - column)
    ramp = jnp.maximum(BW - edge, 0).astype(f32) / BW
    factor = jnp.where(land_v[...] == 1, 0.5, 1.0)
    coef[0] = (1.0 - ramp) * (1.0 - 0.9 * factor)
    coef[1] = (1.0 - ramp) * (0.4 * factor)

    def new_value(x, above, below, sides, mixed, mine, around):
        near = above + below + jnp.asarray(0.125, bf16) * sides
        return mine * x.astype(f32) + around * (near.astype(f32) + 1.25 * mixed)

    def update(r, start, count):
        mixed = jnp.dot(m_v[start : start + count, :], xa[r + 1], preferred_element_type=f32)
        mine, around = coef[0, pl.ds(r, 1), :], coef[1, pl.ds(r, 1), :]
        for s in range(0, count, 16):
            at = slice(start + s, start + s + 16)
            x = xa[r + 1, at, :]
            y = new_value(x, xa[r, at, :], xa[r + 2, at, :], side_sum(x), mixed[s : s + 16], mine, around)
            xb[r + 1, at, :] = y.astype(bf16)

    def first_rows(begin, end):
        def body(i, carry):
            update(2 * i + 1, 0, channels)
            update(2 * i + 2, 0, channels)
            return carry

        lax.fori_loop(begin, end, body, 0)

    row_start, row_end = lax.rem(t, SIDE) == 0, lax.rem(t, SIDE) == SIDE - 1
    beside_row = jnp.logical_or(row_start, row_end)
    strip_early = jnp.logical_or(first, far)
    with jax.named_scope("first_inner"):
        first_rows(0, 3)
    with jax.named_scope("tile_on"):
        pl.when(after_first)(from_below)
        pl.when(jnp.logical_not(row_end))(from_above)
        pl.when(jnp.logical_not(jnp.logical_or(row_start, after_first)))(from_below)


        @pl.when(last)
        def _():
            to_hub[1].start()
            over_up.start()

        @pl.when(after_first)
        def _():
            group_copies[1][1].wait_recv()
            beside_down[0].start()

    with jax.named_scope("first_inner"):
        first_rows(3, (rows - 2) // 2)

    mid, low, high = slice(LANES, width - LANES), slice(0, LANES), slice(width - LANES, width)

    def update_mid(r, start, count):
        mixed = jnp.dot(m_v[start : start + count, :], xb[r + 1, :, mid], preferred_element_type=f32)
        mine, around = coef[0, pl.ds(r, 1), :][:, mid], coef[1, pl.ds(r, 1), :][:, mid]
        for s in range(0, count, 16):
            at = slice(start + s, start + s + 16)
            x = xb[r + 1, at, :]
            sides = side_sum(x)[:, mid]
            y = new_value(x[:, mid], xb[r, at, mid], xb[r + 2, at, mid], sides, mixed[s : s + 16], mine, around)
            xa[r + 1, at, mid] = y.astype(bf16)

    def update_out(r, start, count):
        mixed = jnp.dot(m_v[start : start + count, :], xf[r + 1], preferred_element_type=f32)
        mine, around = [
            jnp.concatenate([row[:, low], row[:, high]], axis=1) for row in (coef[0, pl.ds(r, 1), :], coef[1, pl.ds(r, 1), :])
        ]
        for s in range(0, count, 16):
            at = slice(start + s, start + s + 16)
            x = xf[r + 1, at, :]
            whole = side_sum(jnp.concatenate([x[:, :LANES], xb[r + 1, at, mid], x[:, LANES:]], axis=1))
            sides = jnp.concatenate([whole[:, low], whole[:, high]], axis=1)
            y = new_value(x, xf[r, at, :], xf[r + 2, at, :], sides, mixed[s : s + 16], mine, around)
            y = (y + ws[r, at, :].astype(f32)).astype(bf16)
            xa[r + 1, at, low] = y[:, :LANES]
            xa[r + 1, at, high] = y[:, LANES:]

    def quads(one_row, row, begin, end, start, count):
        def body(i, carry):
            for j in range(4):
                one_row(row + 4 * i + j, start, count)
            return carry

        lax.fori_loop(begin, end, body, 0)

    onward = [
        remote(cand.at[3 * deep + o], cand.at[3 * deep + o], d_send.at[4 + o], d_recv.at[4 + o], to_core) for o in range(3)
    ]

    def deep_tiles():
        @pl.when(jnp.logical_not(after_first))
        def _():
            group_copies[1][1].wait_recv()
            group_copies[0][1].wait_recv()

        onward[1].start()
        onward[0].start()
        group_copies[2][1].wait_recv()
        onward[2].start()

    def middle_quads(begin, end):
        with jax.named_scope("second_middle"):
            quads(update_mid, 2, begin, end, 0, channels)

    early = jnp.where(beside_row, 1, 0)
    sooner = jnp.where(far, 3, early)
    later = jnp.where(far, 3, early + 1)

    def first_edges(c):
        with jax.named_scope("first_halo_wait"):
            halo_arrived(xa, 0, c)
        with jax.named_scope("first_edges"):
            update(0, c * part, part)
            update(rows - 1, c * part, part)

    middle_quads(0, early)
    with jax.named_scope("tile_on"):
        pl.when(jnp.logical_and(row_end, t < tiles - 1))(from_above)
        pl.when(jnp.logical_and(row_start, t > 0))(from_below)

        @pl.when(hub)
        def _():
            pl.semaphore_wait(barrier, 2)
            hub_pass(0)

        @pl.when(first)
        def _():
            pl.semaphore_wait(barrier, 2)
            tile_down.start()
            over_down.start()

    middle_quads(early, sooner)
    first_edges(0)
    with jax.named_scope("tile_on"):

        @pl.when(after_first)
        def _():
            group_copies[0][1].wait_recv()
            beside_down[1].start()

        halo_held(xa, 0, parts - 1)

    halo_start(xb, 1, 0)
    middle_quads(sooner, later)
    with jax.named_scope("deep_tiles_wait"):
        pl.when(hub)(lambda: hub_pass(1))
        pl.when(jnp.logical_and(inside, beside_row))(deep_tiles)
    first_edges(1)
    middle_quads(later, 2)
    with jax.named_scope("deep_tiles_wait"):
        pl.when(jnp.logical_not(beside_row))(deep_tiles)
    middle_quads(jnp.maximum(later, 2), 3)
    with jax.named_scope("tile_on"):
        pl.when(first)(from_below)
        pl.when(last)(from_above)

    cells = 2 * BW
    per = LANES // cells
    short = channels // per

    def pack(begin):
        return jnp.concatenate([strip_v[q * short : (q + 1) * short, begin : begin + cells] for q in range(per)], axis=1)

    ring_up = remote(pack_v.at[0], ring_v.at[0], s_send.at[0], s_recv.at[0], to_up)
    ring_down = remote(pack_v.at[1], ring_v.at[1], s_send.at[1], s_recv.at[1], to_down)

    def boundary_strip():
        with jax.named_scope("deep_tiles_wait"):

            @pl.when(first)
            def _():
                beside_down[0].wait_recv()
                onward[2].start()
                beside_down[1].wait_recv()
                onward[1].start()
                over_up.wait_recv()
                onward[0].start()

            @pl.when(last)
            def _():
                from_hub[0].wait_recv()
                onward[1].start()
                from_hub[1].wait_recv()
                onward[0].start()
                over_down.wait_recv()
                onward[2].start()

        with jax.named_scope("core_tiles_wait"):
            for o in range(3):
                group_copies[o][0].wait_recv()
            for copy in onward:
                copy.wait_recv()
        with jax.named_scope("strip"):
            picked = jnp.concatenate([cand[picks[0, 0, k]] for k in range(slots)], axis=1)
            weights = w_v[...].reshape(slots * LANES, width)
            strip_v[...] = jnp.dot(picked, weights, preferred_element_type=f32).astype(bf16)
        with jax.named_scope("strip_send"):
            pack_v[0] = pack(width - cells)
            pack_v[1] = pack(0)
            pl.when(t < tiles - 1)(ring_up.start)
            pl.when(t > 0)(ring_down.start)
            halo_start(xb, 1, 1)

    def placed(value, j):
        return jnp.dot(value, place_v[j], preferred_element_type=f32)

    def fixed(row, at, wide):
        xf[row, at, :LANES] = (xb[row, at, low].astype(f32) + wide[:, :LANES]).astype(bf16)
        xf[row, at, LANES:] = (xb[row, at, high].astype(f32) + wide[:, LANES:]).astype(bf16)

    everything = slice(0, channels)

    def spread_strip():
        def spread(j, carry):
            value = jnp.concatenate([strip_v[:, b * LANES : (b + 1) * LANES] for b in range(rows // per)], axis=0)
            wide = placed(value, j)
            for b in range(rows // per):
                block = wide[b * channels : (b + 1) * channels]
                ws[per * b + j] = block.astype(bf16)
                fixed(per * b + j + 1, everything, block)
            return carry

        with jax.named_scope("strip_spread"):
            lax.fori_loop(0, per, spread, 0)

    most = channels - part

    def outer_quads(start, count):
        with jax.named_scope("second_outer"):
            quads(update_out, 2, 0, (rows - 4) // 4, start, count)

    def outer_near(start, count):
        with jax.named_scope("second_outer"):
            update_out(1, start, count)
            update_out(rows - 2, start, count)

    w_load.wait()

    pl.when(strip_early)(boundary_strip)

    @pl.when(first)
    def _():
        spread_strip()
        outer_quads(0, most)

    first_edges(parts - 1)
    with jax.named_scope("second_middle"):
        update_mid(1, 0, channels)
        update_mid(rows - 2, 0, channels)
    pl.when(jnp.logical_not(strip_early))(boundary_strip)
    halo_start(xb, 1, parts - 1)

    @pl.when(first)
    def _():
        with jax.named_scope("strip_spread"):
            for r in (0, rows - 1):
                fixed(r + 1, everything, ws[r].astype(f32))

    @pl.when(t > 0)
    def _():
        spread_strip()
        outer_quads(0, most)

    outer_near(0, most)

    for load in av_loads:
        load.wait()
    pool_row = lax.broadcasted_iota(jnp.int32, (width, LANES), 0)
    pool_col = lax.broadcasted_iota(jnp.int32, (width, LANES), 1)
    pool_v[...] = jnp.where(pool_row // 4 == pool_col, 1.0 / 16.0, 0.0).astype(bf16)

    def row_total(begin, count, at):
        total = xa[begin + 1, at, :].astype(f32)
        for j in range(1, count):
            total = total + xa[begin + 1 + j, at, :].astype(f32)
        return total

    def averaged(total):
        return jnp.dot(total.astype(bf16), pool_v[...], preferred_element_type=f32).astype(bf16)

    def feedback_inner(start, count):
        with jax.named_scope("feedback_inner"):
            at = slice(start, start + count)
            tops[0, at] = row_total(1, 3, at)
            tops[1, at] = row_total(rows - 4, 3, at)
            middle = jnp.concatenate([averaged(row_total(4 * b, 4, at)) for b in range(1, bands - 1)], axis=1)
            fb[at] = jnp.dot(middle, av_v[LANES : (bands - 1) * LANES, :], preferred_element_type=f32)

    up_group, down_group = jnp.where(over_above, deep, n), jnp.where(over_below, deep, n)

    def core_copies(c):
        return (
            remote(fbs.at[c, core], r1.at[c, 0], f_send.at[7 * c], f_recv.at[7 * c], to_core),
            remote(fbs.at[c, core_deep], r1.at[c, 1], f_send.at[7 * c + 1], f_recv.at[7 * c + 1], to_core),
        )

    def tile_copy(c, way, k, device):
        i = 7 * c + 2 + 2 * way + k
        return remote(s2.at[c, way, k], r2.at[c, way, k], f_send.at[i], f_recv.at[i], device)

    def down_copies(c):
        return tile_copy(c, 0, 0, to_down), tile_copy(c, 0, 1, (down_group, down))

    def up_copies(c):
        return tile_copy(c, 1, 0, to_up), tile_copy(c, 1, 1, (up_group, up))

    def deep_copy(c):
        return remote(s3.at[c], r3.at[c], f_send.at[7 * c + 6], f_recv.at[7 * c + 6], to_deep)

    def stage_core(c):
        for copy in core_copies(c):
            copy.wait_recv()
        for k, group in enumerate((n, deep)):
            total = fbs[c, group].astype(f32) + r1[c, k].astype(f32)
            s2[c, 0, k] = total[0].astype(bf16)
            s2[c, 1, k] = total[2].astype(bf16)
            g1[c, k] = total[1]
        for copy in (*down_copies(c), *up_copies(c)):
            copy.start()

    def stage_tile(c):
        @pl.when(jnp.logical_not(over_above))
        def _():
            for copy in down_copies(c):
                copy.wait_recv()
            g1[c] = g1[c] + r2[c, 0].astype(f32)

        @pl.when(jnp.logical_not(over_below))
        def _():
            for copy in up_copies(c):
                copy.wait_recv()
            g1[c] = g1[c] + r2[c, 1].astype(f32)

        s3[c] = g1[c, 1].astype(bf16)
        deep_copy(c).start()

    def stage_deep(c):
        @pl.when(over_above)
        def _():
            for copy in down_copies(c):
                copy.wait_recv()
            g1[c, 0] = g1[c, 0] + r2[c, 0, 0].astype(f32) + r2[c, 0, 1].astype(f32)

        @pl.when(over_below)
        def _():
            for copy in up_copies(c):
                copy.wait_recv()
            g1[c, 0] = g1[c, 0] + r2[c, 1, 0].astype(f32) + r2[c, 1, 1].astype(f32)

        deep_copy(c).wait_recv()
        mine = cand[3 * n + 1, span(c), :].astype(f32)
        p_out[span(c), :] = (mine + (g1[c, 0] + r3[c].astype(f32))).astype(bf16)

    def channels_first(c):
        def body(i, carry):
            at = pl.ds(pl.multiple_of(c * part + i * 16, 16), 16)
            x_out[at] = jnp.swapaxes(xa[1 : rows + 1, at, :], 0, 1)
            return carry

        lax.fori_loop(0, part // 16, body, 0)

    feedback_inner(0, most)

    with jax.named_scope("strip_wait"):
        pl.when(t > 0)(ring_up.wait_recv)
        pl.when(t < tiles - 1)(ring_down.wait_recv)

    def halo_strip(c):
        for side, row in ((0, 0), (1, rows + 1)):
            for q in range(per):
                begin, end = max(q * short, c * part), min((q + 1) * short, (c + 1) * part)
                if begin < end:
                    at = slice(begin, end)
                    fixed(row, at, placed(ring_v[side, begin - q * short : end - q * short, :], q))

    for c in range(parts):
        halo_sent(xa, 0, c)
    for c in range(parts):
        if c == parts - 1:
            outer_quads(c * part, part)
            outer_near(c * part, part)
            feedback_inner(c * part, part)
            with jax.named_scope("feedback_core"):
                for k in range(c):
                    stage_core(k)
        with jax.named_scope("second_halo_wait"):
            halo_arrived(xb, 1, c)
        with jax.named_scope("second_edges"):
            halo_strip(c)
            for r in (0, rows - 1):
                update_mid(r, c * part, part)
                update_out(r, c * part, part)
        at = slice(c * part, (c + 1) * part)
        with jax.named_scope("feedback_edges"):
            low_band = averaged(tops[0, at, :] + xa[1, at, :].astype(f32))
            high_band = averaged(tops[1, at, :] + xa[rows, at, :].astype(f32))
            terms = fb[at, :] + jnp.dot(low_band, av_v[:LANES, :], preferred_element_type=f32)
            terms = terms + jnp.dot(high_band, av_v[(bands - 1) * LANES :, :], preferred_element_type=f32)
        with jax.named_scope("feedback_slots"):
            for slot in range(3 * groups):
                total = jnp.zeros((part, LANES), f32)
                for k in range(slots):
                    total = total + (picks[0, 0, k] == slot).astype(f32) * terms[:, k * LANES : (k + 1) * LANES]
                fbs[c, slot // 3, slot % 3] = total.astype(bf16)
            for copy in core_copies(c):
                copy.start()
    with jax.named_scope("channels_first"):
        channels_first(0)
    with jax.named_scope("feedback_core"):
        stage_core(parts - 1)
    with jax.named_scope("channels_first"):
        for c in range(1, parts):
            channels_first(c)
    for c in range(parts):
        with jax.named_scope("feedback_tile"):
            stage_tile(c)
    for c in range(parts):
        with jax.named_scope("feedback_deep"):
            stage_deep(c)

    with jax.named_scope("sent"):
        tile_up.wait_send()
        tile_down.wait_send()
        for copy, _ in group_copies:
            copy.wait_send()

        @pl.when(inside)
        def _():
            for _, copy in group_copies:
                copy.wait_send()

        pl.when(ends)(over_up.wait_send)

        @pl.when(after_first)
        def _():
            for copy in beside_down:
                copy.wait_send()

        @pl.when(last)
        def _():
            for copy in to_hub:
                copy.wait_send()

        @pl.when(hub)
        def _():
            for copy in from_hub:
                copy.wait_send()
        for copy in onward:
            copy.wait_send()
        pl.when(t < tiles - 1)(ring_up.wait_send)
        pl.when(t > 0)(ring_down.wait_send)
        for c in range(parts):
            halo_sent(xb, 1, c)
            for copy in core_copies(c):
                copy.wait_send()
            deep_copy(c).wait_send()
            for copy in (*down_copies(c), *up_copies(c)):
                copy.wait_send()


def write_out(pieces, x, p, nest_out, parent_out, sem):
    size = x.shape[0] // pieces
    copies = [pltpu.make_async_copy(p, parent_out, sem.at[pieces])]
    for c in range(pieces):
        at = pl.ds(c * size, size)
        copies.append(pltpu.make_async_copy(x.at[at], nest_out.at[0, at], sem.at[c]))
    for copy in copies:
        copy.start()
    for copy in copies:
        copy.wait()


def shards(nest_state, parent_state, mix_weight, intersection, interp_weight, avg_weight, land_mask):
    _, channels, rows, width = nest_state.shape
    groups, tiles = lax.axis_size("nest"), lax.axis_size("tile")
    slots = intersection.shape[2]
    cells = parent_state.shape[1]
    parts = 3
    part = channels // parts
    hbm = pl.BlockSpec(memory_space=pl.ANY)
    vmem = pl.BlockSpec(memory_space=pltpu.VMEM)
    x_new, p_new = pl.pallas_call(
        functools.partial(kernel, groups, tiles, parts),
        out_shape=(pltpu.VMEM((channels, rows, width), bf16), pltpu.VMEM((channels, cells), bf16)),
        in_specs=[pl.BlockSpec(memory_space=pltpu.SMEM)] + [hbm] * 6,
        out_specs=(vmem, vmem),
        scratch_shapes=[
            pltpu.VMEM((rows + 2, channels, width), bf16),
            pltpu.VMEM((rows + 2, channels, width), bf16),
            pltpu.VMEM((rows + 2, channels, 2 * LANES), bf16),
            pltpu.VMEM((rows, channels, 2 * LANES), bf16),
            pltpu.VMEM((3 * groups, channels, cells), bf16),
            pltpu.VMEM((2, channels, cells), bf16),
            pltpu.VMEM((channels, channels), bf16),
            pltpu.VMEM((slots, cells, width), bf16),
            pltpu.VMEM((width, slots * cells), bf16),
            pltpu.VMEM((rows, width), jnp.int32),
            pltpu.VMEM((2, rows, width), f32),
            pltpu.VMEM((channels, width), bf16),
            pltpu.VMEM((LANES // (2 * BW), LANES, 2 * LANES), bf16),
            pltpu.VMEM((2, channels * 2 * BW // LANES, LANES), bf16),
            pltpu.VMEM((2, channels * 2 * BW // LANES, LANES), bf16),
            pltpu.VMEM((width, LANES), bf16),
            pltpu.VMEM((2, channels, width), f32),
            pltpu.VMEM((channels, slots * cells), f32),
            pltpu.VMEM((parts, groups, 3, part, cells), bf16),
            pltpu.VMEM((parts, 2, 3, part, cells), bf16),
            pltpu.VMEM((parts, 2, 2, part, cells), bf16),
            pltpu.VMEM((parts, 2, 2, part, cells), bf16),
            pltpu.VMEM((parts, part, cells), bf16),
            pltpu.VMEM((parts, part, cells), bf16),
            pltpu.VMEM((parts, 2, part, cells), f32),
            pltpu.SemaphoreType.DMA((parts + 4 + slots,)),
            pltpu.SemaphoreType.DMA((12,)),
            pltpu.SemaphoreType.DMA((12,)),
            pltpu.SemaphoreType.DMA((7,)),
            pltpu.SemaphoreType.DMA((7,)),
            pltpu.SemaphoreType.DMA((4 * parts,)),
            pltpu.SemaphoreType.DMA((4 * parts,)),
            pltpu.SemaphoreType.DMA((2,)),
            pltpu.SemaphoreType.DMA((2,)),
            pltpu.SemaphoreType.DMA((7 * parts,)),
            pltpu.SemaphoreType.DMA((7 * parts,)),
        ],
        compiler_params=pltpu.CompilerParams(
            collective_id=0, has_side_effects=True, vmem_limit_bytes=48 * 2**20
        ),
    )(intersection, nest_state, parent_state, mix_weight, interp_weight, avg_weight, land_mask)
    return pl.pallas_call(
        functools.partial(write_out, 8),
        out_shape=(
            jax.ShapeDtypeStruct(nest_state.shape, bf16),
            jax.ShapeDtypeStruct(parent_state.shape, bf16),
        ),
        in_specs=[hbm, hbm],
        out_specs=(hbm, hbm),
        scratch_shapes=[pltpu.SemaphoreType.DMA((9,))],
        compiler_params=pltpu.CompilerParams(vmem_limit_bytes=8 * 2**20),
    )(x_new, p_new)


def solution(mesh):
    in_specs = (
        P("nest", None, "tile", None),
        P(None, ("nest", "tile")),
        P(),
        P("nest", "tile", None),
        P("nest", "tile", None, None, None),
        P("nest", "tile", None, None, None),
        P("nest", "tile", None),
    )
    out_specs = (P("nest", None, "tile", None), P(None, ("nest", "tile")))
    return jax.shard_map(shards, mesh=mesh, in_specs=in_specs, out_specs=out_specs, check_vma=False)
```

```python
import functools

import jax
import jax.numpy as jnp
from jax import lax
from jax.experimental import pallas as pl
from jax.experimental.pallas import tpu as pltpu
from jax.sharding import PartitionSpec as P

BW = 16
LANES = 128
SIDE = 4
MESH = pl.DeviceIdType.MESH
f32, bf16 = jnp.float32, jnp.bfloat16


def side_sum(x):
    zero = jnp.zeros((x.shape[0], 1), x.dtype)
    return jnp.concatenate([zero, x[:, :-1]], 1) + jnp.concatenate([x[:, 1:], zero], 1)


def kernel(
    groups, tiles, sizes,
    picks, nest, parent, mix, interp, avg, land,
    x_out, p_out,
    xa, xb, xf, ws, cand, hub_v, m_v, w_v, av_v, land_v, coef, strip_v, place_v, pack_v, ring_v, pool_v, tops, fb, fbs, r1, s2, r2, s3, r3, g1,
    load_sem, p_send, p_recv, d_send, d_recv, h_send, h_recv, s_send, s_recv, f_send, f_recv,
):
    channels, rows, width = x_out.shape
    parts = len(sizes)
    starts = [sum(sizes[:c]) for c in range(parts)]
    slots = w_v.shape[0]
    bands = rows // 4
    n, t = lax.axis_index("nest"), lax.axis_index("tile")
    core = n + 1 - 2 * lax.rem(n, 2)
    deep = lax.rem(n + 2, groups)
    core_deep = lax.rem(core + 2, groups)
    up, down = lax.rem(t + 1, tiles), lax.rem(t + tiles - 1, tiles)
    to_up, to_down, to_core, to_deep = (n, up), (n, down), (core, t), (deep, t)
    first, last = t == 0, t == tiles - 1
    inside = jnp.logical_and(t > 0, t < tiles - 1)
    ends = jnp.logical_or(first, last)
    over_above = jnp.logical_or(t == tiles // 2 - 1, last)
    over_below = jnp.logical_or(t == tiles // 2, first)
    far = jnp.logical_or(t == tiles // 2 - 1, t == tiles // 2)
    hub_tile = tiles // 2 + SIDE - 1
    hub = t == hub_tile

    def remote(src, dst, send, recv, device):
        return pltpu.make_async_remote_copy(
            src_ref=src, dst_ref=dst, send_sem=send, recv_sem=recv, device_id=device, device_id_type=MESH
        )

    barrier = pltpu.get_barrier_semaphore()

    def greet(device):
        pl.semaphore_signal(barrier, inc=1, device_id=device, device_id_type=MESH)

    greet(to_core)
    greet(to_deep)
    pl.when(t < tiles - 1)(lambda: greet(to_up))
    pl.when(t > 0)(lambda: greet(to_down))
    pl.when(t == tiles // 2 - 1)(lambda: greet((deep, up)))
    pl.when(t == tiles // 2)(lambda: greet((deep, down)))

    def span(c):
        return pl.ds(starts[c], sizes[c])

    def held(c):
        return pl.ds(0, sizes[c])

    x_loads = [pltpu.make_async_copy(nest.at[0, span(c)], x_out.at[span(c)], load_sem.at[c]) for c in range(parts)]
    own_load = pltpu.make_async_copy(parent, cand.at[3 * n + 1], load_sem.at[parts])
    mix_load = pltpu.make_async_copy(mix, m_v, load_sem.at[parts + 1])
    land_load = pltpu.make_async_copy(land.at[0], land_v, load_sem.at[parts + 2])
    w_load = pltpu.make_async_copy(interp.at[0, 0], w_v, load_sem.at[parts + 3])
    av_loads = [
        pltpu.make_async_copy(avg.at[0, 0, k], av_v.at[:, k * LANES : (k + 1) * LANES], load_sem.at[parts + 4 + k])
        for k in range(slots)
    ]
    own_load.start()
    for load in x_loads:
        load.start()
    for load in (mix_load, land_load, w_load, *av_loads):
        load.start()
    def rows_first(c):
        x_loads[c].wait()

        def body(i, carry):
            at = pl.ds(pl.multiple_of(starts[c] + i * 16, 16), 16)
            xa[1 : rows + 1, at, :] = jnp.swapaxes(x_out[at], 0, 1)
            return carry

        lax.fori_loop(0, sizes[c] // 16, body, 0)

    @pl.when(first)
    def _():
        pl.semaphore_wait(barrier, 3)
        greet(to_down)
        greet((deep, down))

    @pl.when(jnp.logical_and(inside, jnp.logical_not(far)))
    def _():
        pl.semaphore_wait(barrier, 4)

    @pl.when(far)
    def _():
        pl.semaphore_wait(barrier, 5)

    @pl.when(hub)
    def _():
        greet((n, tiles - 1))
        greet((deep, tiles - 1))

    @pl.when(last)
    def _():
        pl.semaphore_wait(barrier, 7)
        greet(to_up)
        greet((deep, up))
        greet((n, hub_tile))
        greet((deep, hub_tile))

    own_load.wait()
    own = cand.at[3 * n + 1]
    tile_up = remote(own, cand.at[3 * n], p_send.at[0], p_recv.at[0], to_up)
    tile_down = remote(own, cand.at[3 * n + 2], p_send.at[1], p_recv.at[1], to_down)

    def to_groups(o):
        mine = cand.at[3 * n + o]
        return (
            remote(mine, mine, p_send.at[2 + o], p_recv.at[2 + o], to_core),
            remote(mine, mine, p_send.at[5 + o], p_recv.at[5 + o], to_deep),
        )

    group_copies = [to_groups(o) for o in range(3)]

    over_up = remote(own, cand.at[3 * n], p_send.at[9], p_recv.at[9], (deep, up))
    over_down = remote(own, cand.at[3 * n + 2], p_send.at[9], p_recv.at[9], (deep, down))
    def beside(k, source, target, device):
        return remote(cand.at[3 * deep + source], cand.at[3 * deep + target], p_send.at[10 + k], p_recv.at[10 + k], device)

    beside_down = beside(0, 1, 2, to_down), beside(1, 0, 1, to_down)
    after_first = t == 1
    to_hub = [
        remote(cand.at[3 * n + 1 - k], hub_v.at[k], d_send.at[k], d_recv.at[k], (deep, hub_tile)) for k in range(2)
    ]
    from_hub = [
        remote(hub_v.at[k], cand.at[3 * deep + 1 - k], d_send.at[2 + k], d_recv.at[2 + k], (n, tiles - 1))
        for k in range(2)
    ]

    def hub_pass(k):
        to_hub[k].wait_recv()
        from_hub[k].start()

    def pass_on(o):
        group_copies[o][0].start()
        pl.when(inside)(group_copies[o][1].start)

    def from_below():
        tile_up.wait_recv()
        pass_on(0)

    def from_above():
        tile_down.wait_recv()
        pass_on(2)

    with jax.named_scope("own_tile"):
        pl.when(last)(to_hub[0].start)
        tile_up.start()
        pl.when(t > 0)(tile_down.start)
        pass_on(1)

    def halo_up(state, step, c):
        k = (step * parts + c) * 2
        return remote(state.at[rows, span(c)], state.at[0, span(c)], h_send.at[k], h_recv.at[k], to_up)

    def halo_down(state, step, c):
        k = (step * parts + c) * 2 + 1
        return remote(state.at[1, span(c)], state.at[rows + 1, span(c)], h_send.at[k], h_recv.at[k], to_down)

    def halos(state, step, c):
        return halo_up(state, step, c), halo_down(state, step, c)

    def halo_start(state, step, c):
        upward, downward = halos(state, step, c)
        pl.when(t < tiles - 1)(upward.start)
        pl.when(t > 0)(downward.start)

    def halo_one_way(state, step, c):
        upward, downward = halos(state, step, c)
        pl.when(t < tiles - 1)(upward.start)
        pl.when(t > 1)(downward.start)

    def halo_held(state, step, c):
        pl.when(after_first)(halo_down(state, step, c).start)

    def halo_arrived(state, step, c):
        upward, downward = halos(state, step, c)
        pl.when(t > 0)(upward.wait_recv)
        pl.when(t < tiles - 1)(downward.wait_recv)

    def halo_sent(state, step, c):
        upward, downward = halos(state, step, c)
        pl.when(t < tiles - 1)(upward.wait_send)
        pl.when(t > 0)(downward.wait_send)

    @pl.when(first)
    def _():
        ring_v[0] = jnp.zeros(ring_v.shape[1:], bf16)
        for state in (xa, xb):
            state[0] = jnp.zeros((channels, width), bf16)

    @pl.when(last)
    def _():
        ring_v[1] = jnp.zeros(ring_v.shape[1:], bf16)
        for state in (xa, xb):
            state[rows + 1] = jnp.zeros((channels, width), bf16)

    with jax.named_scope("rows_first"):
        for c in range(parts):
            rows_first(c)
            (halo_start if c < parts - 1 else halo_one_way)(xa, 0, c)

    source = lax.broadcasted_iota(jnp.int32, (LANES, 2 * LANES), 0)
    target = lax.broadcasted_iota(jnp.int32, (LANES, 2 * LANES), 1)
    west_at = jnp.where(target < BW, target, -LANES)
    east_at = jnp.where(target >= 2 * LANES - BW, target - (2 * LANES - 2 * BW), -LANES)
    weight = jnp.where(target < BW, BW - target, target - (2 * LANES - BW - 1)).astype(f32) / BW
    for j in range(LANES // (2 * BW)):
        here = source - j * 2 * BW
        place_v[j] = jnp.where((here == west_at) | (here == east_at), weight, 0.0).astype(bf16)

    land_load.wait()
    mix_load.wait()
    m_v[...] = (1.25 * m_v[...].astype(f32)).astype(bf16)
    column = lax.broadcasted_iota(jnp.int32, (rows, width), 1)
    edge = jnp.minimum(column, width - 1 - column)
    ramp = jnp.maximum(BW - edge, 0).astype(f32) / BW
    factor = jnp.where(land_v[...] == 1, 0.5, 1.0)
    coef[0] = (1.0 - ramp) * (1.0 - 0.9 * factor)
    coef[1] = (1.0 - ramp) * (0.4 * factor)

    def new_value(x, above, below, sides, mixed, mine, around):
        near = above + below + jnp.asarray(0.125, bf16) * sides
        return mine * x.astype(f32) + around * (near.astype(f32) + mixed)

    def update(r, start, count):
        mixed = jnp.dot(m_v[start : start + count, :], xa[r + 1], preferred_element_type=f32)
        mine, around = coef[0, pl.ds(r, 1), :], coef[1, pl.ds(r, 1), :]
        for s in range(0, count, 16):
            at = slice(start + s, start + s + 16)
            x = xa[r + 1, at, :]
            y = new_value(x, xa[r, at, :], xa[r + 2, at, :], side_sum(x), mixed[s : s + 16], mine, around)
            xb[r + 1, at, :] = y.astype(bf16)

    def first_rows(begin, end):
        def body(i, carry):
            update(2 * i + 1, 0, channels)
            update(2 * i + 2, 0, channels)
            return carry

        lax.fori_loop(begin, end, body, 0)

    row_start, row_end = lax.rem(t, SIDE) == 0, lax.rem(t, SIDE) == SIDE - 1
    beside_row = jnp.logical_or(row_start, row_end)
    strip_early = jnp.logical_or(first, far)
    with jax.named_scope("first_inner"):
        first_rows(0, 1)
    with jax.named_scope("tile_on"):

        @pl.when(last)
        def _():
            from_below()
            to_hub[1].start()
            over_up.start()

    with jax.named_scope("first_inner"):
        first_rows(1, 3)
    with jax.named_scope("tile_on"):
        pl.when(after_first)(from_below)
        pl.when(jnp.logical_not(row_end))(from_above)
        pl.when(jnp.logical_not(jnp.logical_or(row_start, jnp.logical_or(after_first, last))))(from_below)

        @pl.when(after_first)
        def _():
            group_copies[1][1].wait_recv()
            beside_down[0].start()

    with jax.named_scope("first_inner"):
        first_rows(3, (rows - 2) // 2)

    mid, low, high = slice(LANES, width - LANES), slice(0, LANES), slice(width - LANES, width)

    def update_mid(r, start, count):
        mixed = jnp.dot(m_v[start : start + count, :], xb[r + 1, :, mid], preferred_element_type=f32)
        mine, around = coef[0, pl.ds(r, 1), :][:, mid], coef[1, pl.ds(r, 1), :][:, mid]
        for s in range(0, count, 16):
            at = slice(start + s, start + s + 16)
            x = xb[r + 1, at, :]
            sides = side_sum(x)[:, mid]
            y = new_value(x[:, mid], xb[r, at, mid], xb[r + 2, at, mid], sides, mixed[s : s + 16], mine, around)
            xa[r + 1, at, mid] = y.astype(bf16)

    def update_out(r, start, count):
        mixed = jnp.dot(m_v[start : start + count, :], xf[r + 1], preferred_element_type=f32)
        mine, around = [
            jnp.concatenate([row[:, low], row[:, high]], axis=1) for row in (coef[0, pl.ds(r, 1), :], coef[1, pl.ds(r, 1), :])
        ]
        for s in range(0, count, 16):
            at = slice(start + s, start + s + 16)
            x = xf[r + 1, at, :]
            whole = side_sum(jnp.concatenate([x[:, :LANES], xb[r + 1, at, mid], x[:, LANES:]], axis=1))
            sides = jnp.concatenate([whole[:, low], whole[:, high]], axis=1)
            y = new_value(x, xf[r, at, :], xf[r + 2, at, :], sides, mixed[s : s + 16], mine, around)
            y = (y + ws[r, at, :].astype(f32)).astype(bf16)
            xa[r + 1, at, low] = y[:, :LANES]
            xa[r + 1, at, high] = y[:, LANES:]

    def quads(one_row, row, begin, end, start, count):
        def body(i, carry):
            for j in range(4):
                one_row(row + 4 * i + j, start, count)
            return carry

        lax.fori_loop(begin, end, body, 0)

    onward = [
        remote(cand.at[3 * deep + o], cand.at[3 * deep + o], d_send.at[4 + o], d_recv.at[4 + o], to_core) for o in range(3)
    ]

    def deep_tiles():
        @pl.when(jnp.logical_not(after_first))
        def _():
            group_copies[1][1].wait_recv()
            group_copies[0][1].wait_recv()

        onward[1].start()
        onward[0].start()
        group_copies[2][1].wait_recv()
        onward[2].start()

    def middle_quads(begin, end):
        with jax.named_scope("second_middle"):
            quads(update_mid, 2, begin, end, 0, channels)

    early = jnp.where(beside_row, 1, 0)
    sooner = jnp.where(far, 3, early)
    later = jnp.where(far, 3, early + 1)

    def first_edges(c):
        with jax.named_scope("first_halo_wait"):
            halo_arrived(xa, 0, c)
        with jax.named_scope("first_edges"):
            update(0, starts[c], sizes[c])
            update(rows - 1, starts[c], sizes[c])

    @pl.when(first)
    def _():
        pl.semaphore_wait(barrier, 2)
        tile_down.start()
        over_down.start()

    middle_quads(0, early)
    with jax.named_scope("tile_on"):
        pl.when(jnp.logical_and(row_end, t < tiles - 1))(from_above)
        pl.when(jnp.logical_and(row_start, t > 0))(from_below)

        @pl.when(hub)
        def _():
            pl.semaphore_wait(barrier, 2)
            hub_pass(0)

    middle_quads(early, sooner)
    first_edges(0)
    with jax.named_scope("tile_on"):

        @pl.when(after_first)
        def _():
            group_copies[0][1].wait_recv()
            beside_down[1].start()

        halo_held(xa, 0, parts - 1)

    halo_start(xb, 1, 0)
    middle_quads(sooner, later)
    with jax.named_scope("deep_tiles_wait"):
        pl.when(hub)(lambda: hub_pass(1))
        pl.when(jnp.logical_and(inside, beside_row))(deep_tiles)
    first_edges(1)
    middle_quads(later, 2)
    with jax.named_scope("deep_tiles_wait"):
        pl.when(jnp.logical_not(beside_row))(deep_tiles)
    middle_quads(jnp.maximum(later, 2), 3)
    with jax.named_scope("tile_on"):
        pl.when(first)(from_below)

        @pl.when(last)
        def _():
            from_above()
            over_down.wait_recv()
            onward[2].start()
            from_hub[0].wait_recv()
            onward[1].start()


    cells = 2 * BW
    per = LANES // cells
    short = channels // per

    def pack(begin):
        return jnp.concatenate([strip_v[q * short : (q + 1) * short, begin : begin + cells] for q in range(per)], axis=1)

    ring_up = remote(pack_v.at[0], ring_v.at[0], s_send.at[0], s_recv.at[0], to_up)
    ring_down = remote(pack_v.at[1], ring_v.at[1], s_send.at[1], s_recv.at[1], to_down)

    def boundary_strip():
        with jax.named_scope("deep_tiles_wait"):

            @pl.when(first)
            def _():
                beside_down[0].wait_recv()
                onward[2].start()
                beside_down[1].wait_recv()
                onward[1].start()
                over_up.wait_recv()
                onward[0].start()

            @pl.when(last)
            def _():
                from_hub[1].wait_recv()
                onward[0].start()

        with jax.named_scope("core_tiles_wait"):
            for o in range(3):
                group_copies[o][0].wait_recv()
            for copy in onward:
                copy.wait_recv()
        with jax.named_scope("strip"):
            picked = jnp.concatenate([cand[picks[0, 0, k]] for k in range(slots)], axis=1)
            weights = w_v[...].reshape(slots * LANES, width)
            strip_v[...] = jnp.dot(picked, weights, preferred_element_type=f32).astype(bf16)
        with jax.named_scope("strip_send"):
            pack_v[0] = pack(width - cells)
            pack_v[1] = pack(0)
            pl.when(t < tiles - 1)(ring_up.start)
            pl.when(t > 0)(ring_down.start)
            halo_start(xb, 1, 1)

    def placed(value, j):
        return jnp.dot(value, place_v[j], preferred_element_type=f32)

    def fixed(row, at, wide):
        xf[row, at, :LANES] = (xb[row, at, low].astype(f32) + wide[:, :LANES]).astype(bf16)
        xf[row, at, LANES:] = (xb[row, at, high].astype(f32) + wide[:, LANES:]).astype(bf16)

    everything = slice(0, channels)

    def spread_strip():
        def spread(j, carry):
            value = jnp.concatenate([strip_v[:, b * LANES : (b + 1) * LANES] for b in range(rows // per)], axis=0)
            wide = placed(value, j)
            for b in range(rows // per):
                block = wide[b * channels : (b + 1) * channels]
                ws[per * b + j] = block.astype(bf16)
                fixed(per * b + j + 1, everything, block)
            return carry

        with jax.named_scope("strip_spread"):
            lax.fori_loop(0, per, spread, 0)

    most = starts[-1]

    def outer_quads(start, count):
        with jax.named_scope("second_outer"):
            quads(update_out, 2, 0, (rows - 4) // 4, start, count)

    def outer_near(start, count):
        with jax.named_scope("second_outer"):
            update_out(1, start, count)
            update_out(rows - 2, start, count)

    w_load.wait()

    pl.when(strip_early)(boundary_strip)

    @pl.when(first)
    def _():
        spread_strip()
        outer_quads(0, most)

    first_edges(parts - 1)
    with jax.named_scope("second_middle"):
        update_mid(1, 0, channels)
        update_mid(rows - 2, 0, channels)
    pl.when(jnp.logical_not(strip_early))(boundary_strip)
    halo_start(xb, 1, parts - 1)

    @pl.when(first)
    def _():
        with jax.named_scope("strip_spread"):
            for r in (0, rows - 1):
                fixed(r + 1, everything, ws[r].astype(f32))

    @pl.when(t > 0)
    def _():
        spread_strip()
        outer_quads(0, most)

    outer_near(0, most)

    for load in av_loads:
        load.wait()
    pool_row = lax.broadcasted_iota(jnp.int32, (width, LANES), 0)
    pool_col = lax.broadcasted_iota(jnp.int32, (width, LANES), 1)
    pool_v[...] = jnp.where(pool_row // 4 == pool_col, 1.0 / 16.0, 0.0).astype(bf16)

    def row_total(begin, count, at):
        total = xa[begin + 1, at, :].astype(f32)
        for j in range(1, count):
            total = total + xa[begin + 1 + j, at, :].astype(f32)
        return total

    def averaged(total):
        return jnp.dot(total.astype(bf16), pool_v[...], preferred_element_type=f32).astype(bf16)

    def feedback_inner(start, count):
        with jax.named_scope("feedback_inner"):
            at = slice(start, start + count)
            tops[0, at] = row_total(1, 3, at)
            tops[1, at] = row_total(rows - 4, 3, at)
            middle = jnp.concatenate([averaged(row_total(4 * b, 4, at)) for b in range(1, bands - 1)], axis=1)
            fb[at] = jnp.dot(middle, av_v[LANES : (bands - 1) * LANES, :], preferred_element_type=f32)

    up_group, down_group = jnp.where(over_above, deep, n), jnp.where(over_below, deep, n)

    def core_copy(c, k, group):
        i = 7 * c + k
        blocks, landing = fbs.at[c, group, :, held(c)], r1.at[c, k, :, held(c)]
        return remote(blocks, landing, f_send.at[i], f_recv.at[i], to_core)

    def core_copies(c):
        return core_copy(c, 0, core), core_copy(c, 1, core_deep)

    def tile_copy(c, way, k, device):
        i = 7 * c + 2 + 2 * way + k
        return remote(s2.at[c, way, k, held(c)], r2.at[c, way, k, held(c)], f_send.at[i], f_recv.at[i], device)

    def down_copies(c):
        return tile_copy(c, 0, 0, to_down), tile_copy(c, 0, 1, (down_group, down))

    def up_copies(c):
        return tile_copy(c, 1, 0, to_up), tile_copy(c, 1, 1, (up_group, up))

    def deep_copy(c):
        return remote(s3.at[c, held(c)], r3.at[c, held(c)], f_send.at[7 * c + 6], f_recv.at[7 * c + 6], to_deep)

    def stage_core(c):
        for copy in core_copies(c):
            copy.wait_recv()
        for k, group in enumerate((n, deep)):
            total = fbs[c, group, :, held(c)].astype(f32) + r1[c, k, :, held(c)].astype(f32)
            s2[c, 0, k, held(c)] = total[0].astype(bf16)
            s2[c, 1, k, held(c)] = total[2].astype(bf16)
            g1[c, k, held(c)] = total[1]
        for copy in (*down_copies(c), *up_copies(c)):
            copy.start()

    def stage_tile(c):
        at = held(c)

        @pl.when(jnp.logical_not(over_above))
        def _():
            for copy in down_copies(c):
                copy.wait_recv()
            g1[c, :, at] = g1[c, :, at] + r2[c, 0, :, at].astype(f32)

        @pl.when(jnp.logical_not(over_below))
        def _():
            for copy in up_copies(c):
                copy.wait_recv()
            g1[c, :, at] = g1[c, :, at] + r2[c, 1, :, at].astype(f32)

        s3[c, at] = g1[c, 1, at].astype(bf16)
        deep_copy(c).start()

    def stage_deep(c):
        at = held(c)

        @pl.when(over_above)
        def _():
            for copy in down_copies(c):
                copy.wait_recv()
            g1[c, 0, at] = g1[c, 0, at] + r2[c, 0, 0, at].astype(f32) + r2[c, 0, 1, at].astype(f32)

        @pl.when(over_below)
        def _():
            for copy in up_copies(c):
                copy.wait_recv()
            g1[c, 0, at] = g1[c, 0, at] + r2[c, 1, 0, at].astype(f32) + r2[c, 1, 1, at].astype(f32)

        deep_copy(c).wait_recv()
        mine = cand[3 * n + 1, span(c), :].astype(f32)
        p_out[span(c), :] = (mine + (g1[c, 0, at] + r3[c, at].astype(f32))).astype(bf16)

    def channels_first(c):
        def body(i, carry):
            at = pl.ds(pl.multiple_of(starts[c] + i * 16, 16), 16)
            x_out[at] = jnp.swapaxes(xa[1 : rows + 1, at, :], 0, 1)
            return carry

        lax.fori_loop(0, sizes[c] // 16, body, 0)

    feedback_inner(0, most)

    with jax.named_scope("strip_wait"):
        pl.when(t > 0)(ring_up.wait_recv)
        pl.when(t < tiles - 1)(ring_down.wait_recv)

    def halo_strip(c):
        for side, row in ((0, 0), (1, rows + 1)):
            for q in range(per):
                begin, end = max(q * short, starts[c]), min((q + 1) * short, starts[c] + sizes[c])
                if begin < end:
                    at = slice(begin, end)
                    fixed(row, at, placed(ring_v[side, begin - q * short : end - q * short, :], q))

    for c in range(parts):
        halo_sent(xa, 0, c)
    def last_part():
        outer_quads(starts[-1], sizes[-1])
        outer_near(starts[-1], sizes[-1])
        feedback_inner(starts[-1], sizes[-1])

    for c in range(parts):
        if c == 1:
            pl.when(far)(last_part)
        if c == parts - 1:
            pl.when(jnp.logical_not(far))(last_part)
            with jax.named_scope("feedback_core"):
                stage_core(0)
                pl.when(jnp.logical_not(far))(lambda: stage_core(1))
        with jax.named_scope("second_halo_wait"):
            halo_arrived(xb, 1, c)
        with jax.named_scope("second_edges"):
            halo_strip(c)
            for r in (0, rows - 1):
                update_mid(r, starts[c], sizes[c])
                update_out(r, starts[c], sizes[c])
        at = slice(starts[c], starts[c] + sizes[c])
        with jax.named_scope("feedback_edges"):
            low_band = averaged(tops[0, at, :] + xa[1, at, :].astype(f32))
            high_band = averaged(tops[1, at, :] + xa[rows, at, :].astype(f32))
            terms = fb[at, :] + jnp.dot(low_band, av_v[:LANES, :], preferred_element_type=f32)
            terms = terms + jnp.dot(high_band, av_v[(bands - 1) * LANES :, :], preferred_element_type=f32)
        with jax.named_scope("feedback_slots"):
            for slot in range(3 * groups):
                total = jnp.zeros((sizes[c], LANES), f32)
                for k in range(slots):
                    total = total + (picks[0, 0, k] == slot).astype(f32) * terms[:, k * LANES : (k + 1) * LANES]
                fbs[c, slot // 3, slot % 3, held(c)] = total.astype(bf16)
            for copy in core_copies(c):
                copy.start()
    with jax.named_scope("feedback_core"):
        pl.when(far)(lambda: stage_core(1))
    with jax.named_scope("channels_first"):
        channels_first(0)
    with jax.named_scope("feedback_core"):
        stage_core(parts - 1)
    with jax.named_scope("channels_first"):
        for c in range(1, parts):
            channels_first(c)
    for c in range(parts):
        with jax.named_scope("feedback_tile"):
            stage_tile(c)
    for c in range(parts):
        with jax.named_scope("feedback_deep"):
            stage_deep(c)

    with jax.named_scope("sent"):
        tile_up.wait_send()
        tile_down.wait_send()
        for copy, _ in group_copies:
            copy.wait_send()

        @pl.when(inside)
        def _():
            for _, copy in group_copies:
                copy.wait_send()

        pl.when(ends)(over_up.wait_send)

        @pl.when(after_first)
        def _():
            for copy in beside_down:
                copy.wait_send()

        @pl.when(last)
        def _():
            for copy in to_hub:
                copy.wait_send()

        @pl.when(hub)
        def _():
            for copy in from_hub:
                copy.wait_send()
        for copy in onward:
            copy.wait_send()
        pl.when(t < tiles - 1)(ring_up.wait_send)
        pl.when(t > 0)(ring_down.wait_send)
        for c in range(parts):
            halo_sent(xb, 1, c)
            for copy in core_copies(c):
                copy.wait_send()
            deep_copy(c).wait_send()
            for copy in (*down_copies(c), *up_copies(c)):
                copy.wait_send()


def write_out(pieces, x, p, nest_out, parent_out, sem):
    size = x.shape[0] // pieces
    copies = [pltpu.make_async_copy(p, parent_out, sem.at[pieces])]
    for c in range(pieces):
        at = pl.ds(c * size, size)
        copies.append(pltpu.make_async_copy(x.at[at], nest_out.at[0, at], sem.at[c]))
    for copy in copies:
        copy.start()
    for copy in copies:
        copy.wait()


def shards(nest_state, parent_state, mix_weight, intersection, interp_weight, avg_weight, land_mask):
    _, channels, rows, width = nest_state.shape
    groups, tiles = lax.axis_size("nest"), lax.axis_size("tile")
    slots = intersection.shape[2]
    cells = parent_state.shape[1]
    sizes = (channels // 3,) * 3
    parts, part = len(sizes), max(sizes)
    hbm = pl.BlockSpec(memory_space=pl.ANY)
    vmem = pl.BlockSpec(memory_space=pltpu.VMEM)
    x_new, p_new = pl.pallas_call(
        functools.partial(kernel, groups, tiles, sizes),
        out_shape=(pltpu.VMEM((channels, rows, width), bf16), pltpu.VMEM((channels, cells), bf16)),
        in_specs=[pl.BlockSpec(memory_space=pltpu.SMEM)] + [hbm] * 6,
        out_specs=(vmem, vmem),
        scratch_shapes=[
            pltpu.VMEM((rows + 2, channels, width), bf16),
            pltpu.VMEM((rows + 2, channels, width), bf16),
            pltpu.VMEM((rows + 2, channels, 2 * LANES), bf16),
            pltpu.VMEM((rows, channels, 2 * LANES), bf16),
            pltpu.VMEM((3 * groups, channels, cells), bf16),
            pltpu.VMEM((2, channels, cells), bf16),
            pltpu.VMEM((channels, channels), bf16),
            pltpu.VMEM((slots, cells, width), bf16),
            pltpu.VMEM((width, slots * cells), bf16),
            pltpu.VMEM((rows, width), jnp.int32),
            pltpu.VMEM((2, rows, width), f32),
            pltpu.VMEM((channels, width), bf16),
            pltpu.VMEM((LANES // (2 * BW), LANES, 2 * LANES), bf16),
            pltpu.VMEM((2, channels * 2 * BW // LANES, LANES), bf16),
            pltpu.VMEM((2, channels * 2 * BW // LANES, LANES), bf16),
            pltpu.VMEM((width, LANES), bf16),
            pltpu.VMEM((2, channels, width), f32),
            pltpu.VMEM((channels, slots * cells), f32),
            pltpu.VMEM((parts, groups, 3, part, cells), bf16),
            pltpu.VMEM((parts, 2, 3, part, cells), bf16),
            pltpu.VMEM((parts, 2, 2, part, cells), bf16),
            pltpu.VMEM((parts, 2, 2, part, cells), bf16),
            pltpu.VMEM((parts, part, cells), bf16),
            pltpu.VMEM((parts, part, cells), bf16),
            pltpu.VMEM((parts, 2, part, cells), f32),
            pltpu.SemaphoreType.DMA((parts + 4 + slots,)),
            pltpu.SemaphoreType.DMA((12,)),
            pltpu.SemaphoreType.DMA((12,)),
            pltpu.SemaphoreType.DMA((7,)),
            pltpu.SemaphoreType.DMA((7,)),
            pltpu.SemaphoreType.DMA((4 * parts,)),
            pltpu.SemaphoreType.DMA((4 * parts,)),
            pltpu.SemaphoreType.DMA((2,)),
            pltpu.SemaphoreType.DMA((2,)),
            pltpu.SemaphoreType.DMA((7 * parts,)),
            pltpu.SemaphoreType.DMA((7 * parts,)),
        ],
        compiler_params=pltpu.CompilerParams(
            collective_id=0, has_side_effects=True, vmem_limit_bytes=48 * 2**20
        ),
    )(intersection, nest_state, parent_state, mix_weight, interp_weight, avg_weight, land_mask)
    return pl.pallas_call(
        functools.partial(write_out, 8),
        out_shape=(
            jax.ShapeDtypeStruct(nest_state.shape, bf16),
            jax.ShapeDtypeStruct(parent_state.shape, bf16),
        ),
        in_specs=[hbm, hbm],
        out_specs=(hbm, hbm),
        scratch_shapes=[pltpu.SemaphoreType.DMA((9,))],
        compiler_params=pltpu.CompilerParams(vmem_limit_bytes=8 * 2**20),
    )(x_new, p_new)


def solution(mesh):
    in_specs = (
        P("nest", None, "tile", None),
        P(None, ("nest", "tile")),
        P(),
        P("nest", "tile", None),
        P("nest", "tile", None, None, None),
        P("nest", "tile", None, None, None),
        P("nest", "tile", None),
    )
    out_specs = (P("nest", None, "tile", None), P(None, ("nest", "tile")))
    return jax.shard_map(shards, mesh=mesh, in_specs=in_specs, out_specs=out_specs, check_vma=False)
```
